32 devices in a mesh: region: 2 (over y), tile: 4 (over z), sub: 2 (over x), lane: 2 (over core).
Axes of the slice: x: 2, y: 2, z: 4, core: 2. Of those that a mesh axis runs over, the one named last changes fastest.
Arguments:
- state: float32 [3, 64, 128, 128], P(None, ('region', 'tile', 'sub', 'lane')), parts along dimension 1, may hold values from -5.04 to 5.04, as said below
- terrain_local: bfloat16 [2, 64, 128, 128], P(None, ('region', 'tile', 'sub', 'lane')), parts along dimension 1, may hold values from -0.9 to 0.9, as said below
- terrain_store: bfloat16 [2, 128, 128, 128], P(None, ('region', 'tile', 'sub', 'lane')), parts along dimension 1, may hold values from -0.9 to 0.9, as said below
- wet_count: int32 [32], P(('region', 'tile', 'sub', 'lane')), parts along dimension 0, may hold values from 1 to 2, as said below
- face_links: int32 [64, 2, 4], P(('region', 'tile', 'sub', 'lane')), parts along dimension 0, may hold values from -1 to 15, as said below
- new_source: int32 [64], P(('region', 'tile', 'sub', 'lane')), parts along dimension 0, may hold values from -1 to 3, as said below
- store_target: int32 [128], P(('region', 'tile', 'sub', 'lane')), parts along dimension 0, may hold values from -1 to 3, as said below
Outputs:
- state_out: float32 [3, 64, 128, 128], P(None, ('region', 'tile', 'sub', 'lane')), parts along dimension 1
The draws below stay inside these ranges and needn't reach their ends.
There are 2 independent parts, one for each index of `region`. The reference program is written for one: setup_inputs(seed, part) draws one part's arguments, and reference() takes and returns one part's arrays. A program takes and returns all parts, laid end to end along the dimension named above; each array names one. Nothing has to cross between parts.
Inputs may be any that keep to these rules, and one draw needn't show every extreme that they name: state[0] is a water depth of 0.7 to 4.2; the discharges state[1] and state[2] are at most 1.2 times the depth in magnitude. terrain_local[0] is a bed elevation, terrain_local[1] a Manning coefficient of 0.03 to 0.3. terrain_store[0] is a bed elevation, terrain_store[1] a Manning coefficient of 0.03 to 0.3. A device's live tiles fill its first wet_count slots, the other slots are padding; some device has 2. `face_links`: [i, 0, f] is the device and [i, 1, f] the slot of the live tile across face f of tile i, both -1 where the face is a wall or i is padding; links are mutual (west with east, north with south); across west or east faces the device has the same tile index, across a north face a tile index one lower, across a south face one higher; the tiles of one device have at most 1 face of one direction linked to tiles of any one device, and some device has that many. `new_source`: -1 for live tiles that were wet before and for padding; for a newly wetted tile the tile index of the device that stores its terrain, which has the same sub and lane indices; no two new tiles of one device come from the same device; a device has at most 2 new tiles, and some device has that many. `store_target`: for each stored block, the tile index of the device (same sub and lane) whose new tile asks for it, or -1; every request of new_source names exactly one block of the storing device.
All inputs are finite; a program needn't handle non-finite values.
Results may differ from the reference program's by a relative error of at most 0.0004.
Values may be sent and summed in bfloat16 or wider, within the bound.
A program may use at most 64 MiB of HBM per device.

```python
import math
import jax
import jax.numpy as jnp
from jax import lax

TS = 128
SLOTS = 2
STEPS = 3
N_TILE = 4
N_SUB = 2
N_LANE = 2


def permutations(subkey, count, length):
    return jax.vmap(lambda single: jax.random.permutation(single, length))(jax.random.split(subkey, count))


def layout(key):
    peer_count = N_SUB * N_LANE
    band_count = N_TILE
    device_total = band_count * peer_count
    most_new = min(SLOTS, N_TILE)
    subkeys = [jax.random.fold_in(key, 100 + offset) for offset in range(12)]
    slot_ids = jnp.arange(SLOTS, dtype=jnp.int32)
    band_grid = jnp.arange(band_count, dtype=jnp.int32)[:, None, None]
    peer_grid = jnp.arange(peer_count, dtype=jnp.int32)[None, :, None]
    slot_grid = slot_ids[None, None, :]
    front = jax.random.randint(subkeys[0], (band_count, peer_count), 0, 4) == 0
    chosen = jax.random.randint(subkeys[1], (), 0, device_total)
    front = front | (jnp.arange(device_total).reshape(band_count, peer_count) == chosen)
    wet = jnp.where(front, SLOTS, jax.random.randint(subkeys[2], (band_count, peer_count), max(1, SLOTS // 2), SLOTS + 1)).astype(jnp.int32)
    live = slot_grid < wet[:, :, None]
    east_shift = permutations(subkeys[3], band_count, peer_count)[:, slot_ids % peer_count]
    west_slot = permutations(subkeys[4], device_total, SLOTS).reshape(band_count, peer_count, SLOTS)
    west_anchor = jnp.argsort(west_slot, axis=2).astype(jnp.int32)
    north_shift = permutations(subkeys[5], band_count, peer_count)[:, slot_ids % peer_count]
    south_slot = permutations(subkeys[6], device_total, SLOTS).reshape(band_count, peer_count, SLOTS)
    south_anchor = jnp.argsort(south_slot, axis=2).astype(jnp.int32)
    east_peer = (peer_grid + east_shift[:, None, :]) % peer_count
    east_slot = west_slot[band_grid, east_peer, slot_grid]
    east_valid = live & live[band_grid, east_peer, east_slot]
    east_device = band_grid * peer_count + east_peer
    west_peer = (peer_grid - east_shift[band_grid, west_anchor]) % peer_count
    west_valid = live & live[band_grid, west_peer, west_anchor]
    west_device = band_grid * peer_count + west_peer
    upper_band = jnp.maximum(band_grid - 1, 0)
    north_peer = (peer_grid + north_shift[:, None, :]) % peer_count
    north_slot = south_slot[upper_band, north_peer, slot_grid]
    north_valid = live & (band_grid > 0) & live[upper_band, north_peer, north_slot]
    north_device = upper_band * peer_count + north_peer
    lower_band = jnp.minimum(band_grid + 1, band_count - 1)
    south_peer = (peer_grid - north_shift[lower_band, south_anchor]) % peer_count
    south_valid = live & (band_grid < band_count - 1) & live[lower_band, south_peer, south_anchor]
    south_device = lower_band * peer_count + south_peer
    valid_all = jnp.stack([west_valid, east_valid, north_valid, south_valid], axis=-1)
    device_all = jnp.where(valid_all, jnp.stack([west_device, east_device, north_device, south_device], axis=-1), -1)
    slot_all = jnp.where(valid_all, jnp.stack([west_anchor, east_slot, north_slot, south_anchor], axis=-1), -1)
    face_links = jnp.stack([device_all, slot_all], axis=3).reshape(device_total * SLOTS, 2, 4).astype(jnp.int32)
    ordering = permutations(subkeys[7], device_total, SLOTS).reshape(band_count, peer_count, SLOTS)
    smaller = (ordering[:, :, None, :] < ordering[:, :, :, None]) & live[:, :, None, :]
    live_rank = jnp.sum(smaller.astype(jnp.int32), axis=3)
    other_new = jnp.minimum(jax.random.randint(subkeys[8], (band_count, peer_count), 0, most_new // 2 + 1), wet)
    new_count = jnp.where(front, most_new, other_new)
    fresh = live & (live_rank < new_count[:, :, None])
    sources = permutations(subkeys[9], device_total, N_TILE).reshape(band_count, peer_count, N_TILE)
    picked = jnp.take_along_axis(sources, jnp.minimum(live_rank, N_TILE - 1), axis=2)
    new_source = jnp.where(fresh, picked, -1).astype(jnp.int32)
    asked = jnp.any(new_source[None, :, :, :] == jnp.arange(band_count)[:, None, None, None], axis=3)
    asked = jnp.transpose(asked, (0, 2, 1))
    block_order = permutations(subkeys[10], device_total, N_TILE).reshape(band_count, peer_count, N_TILE)
    matches = (block_order[:, :, :, None] == jnp.arange(N_TILE)[None, None, None, :]) & asked[:, :, :, None]
    store_target = jnp.sum(jnp.where(matches, jnp.arange(band_count)[None, None, :, None] + 1, 0), axis=2) - 1
    return (wet.reshape(-1), face_links, new_source.reshape(-1), store_target.reshape(-1).astype(jnp.int32))


def draw_wet_count(key, part):
    shared = layout(key)
    return shared[0]


def draw_face_links(key, part):
    shared = layout(key)
    return shared[1]


def draw_new_source(key, part):
    shared = layout(key)
    return shared[2]


def draw_store_target(key, part):
    shared = layout(key)
    return shared[3]


def draw_state(key, part):
    key = jax.random.fold_in(key, 5)
    key_base, key_cell, key_flow = jax.random.split(key, 3)
    tile_total = SLOTS * N_TILE * N_SUB * N_LANE
    base = jnp.exp(jax.random.uniform(key_base, (1, tile_total, 1, 1), minval=0.0, maxval=math.log(3.0)))
    cell = jnp.exp(jax.random.uniform(key_cell, (1, tile_total, TS, TS), minval=math.log(0.7), maxval=math.log(1.4)))
    flow = 0.4 * jax.random.truncated_normal(key_flow, -3.0, 3.0, (2, tile_total, TS, TS))
    depth = base * cell
    return jnp.concatenate([depth, depth * flow], axis=0).astype(jnp.float32)


def draw_terrain_local(key, part):
    key = jax.random.fold_in(key, 6)
    key_bed = jax.random.fold_in(key, 0)
    key_rough = jax.random.fold_in(key, 2)
    count = SLOTS * N_TILE * N_SUB * N_LANE
    bed_level = 0.25 * jax.random.truncated_normal(key_bed, -3.0, 3.0, (1, count, TS, TS))
    roughness = jnp.exp(jax.random.uniform(key_rough, (1, count, TS, TS), minval=math.log(0.03), maxval=math.log(0.3)))
    return jnp.concatenate([bed_level, roughness], axis=0).astype(jnp.bfloat16)


def draw_terrain_store(key, part):
    key = jax.random.fold_in(key, 7)
    key_bed = jax.random.fold_in(key, 0)
    key_rough = jax.random.fold_in(key, 2)
    count = N_TILE * N_TILE * N_SUB * N_LANE
    bed_level = 0.25 * jax.random.truncated_normal(key_bed, -3.0, 3.0, (1, count, TS, TS))
    roughness = jnp.exp(jax.random.uniform(key_rough, (1, count, TS, TS), minval=math.log(0.03), maxval=math.log(0.3)))
    return jnp.concatenate([bed_level, roughness], axis=0).astype(jnp.bfloat16)


def setup_inputs(seed: int = 0, part: int = 0) -> dict:
    arg_keys = jax.random.split(jax.random.key(seed), 8)
    own_keys = jax.random.split(jax.random.fold_in(arg_keys[7], part), 8)
    state = draw_state(jax.random.fold_in(jax.random.fold_in(arg_keys[7], part), 71), part)
    terrain_local = draw_terrain_local(jax.random.fold_in(jax.random.fold_in(arg_keys[7], part), 71), part)
    terrain_store = draw_terrain_store(jax.random.fold_in(jax.random.fold_in(arg_keys[7], part), 71), part)
    wet_count = draw_wet_count(jax.random.fold_in(jax.random.fold_in(arg_keys[7], part), 71), part)
    face_links = draw_face_links(jax.random.fold_in(jax.random.fold_in(arg_keys[7], part), 71), part)
    new_source = draw_new_source(jax.random.fold_in(jax.random.fold_in(arg_keys[7], part), 71), part)
    store_target = draw_store_target(jax.random.fold_in(jax.random.fold_in(arg_keys[7], part), 71), part)
    return {"state": state, "terrain_local": terrain_local, "terrain_store": terrain_store, "wet_count": wet_count, "face_links": face_links, "new_source": new_source, "store_target": store_target}


gravity_accel = 9.81
cell_width = 30.0
time_step = 1.0
mirror_signs = ((1.0, -1.0, 1.0, 1.0), (1.0, -1.0, 1.0, 1.0), (1.0, 1.0, -1.0, 1.0), (1.0, 1.0, -1.0, 1.0))
opposite_face = (1, 0, 3, 2)

def face_flux(depth_left, normal_left, tangent_left, level_left, depth_right, normal_right, tangent_right, level_right):
    level_face = jnp.maximum(level_left, level_right)
    held_left = jnp.maximum(depth_left + level_left - level_face, 0.0)
    held_right = jnp.maximum(depth_right + level_right - level_face, 0.0)
    speed_left = normal_left / depth_left
    speed_right = normal_right / depth_right
    drift_left = tangent_left / depth_left
    drift_right = tangent_right / depth_right
    wave_speed = jnp.maximum(jnp.abs(speed_left) + jnp.sqrt(gravity_accel * held_left), jnp.abs(speed_right) + jnp.sqrt(gravity_accel * held_right))
    push_left = held_left * speed_left * speed_left + 0.5 * gravity_accel * held_left * held_left
    push_right = held_right * speed_right * speed_right + 0.5 * gravity_accel * held_right * held_right
    mass_flux = 0.5 * (held_left * speed_left + held_right * speed_right) - 0.5 * wave_speed * (held_right - held_left)
    normal_flux = 0.5 * (push_left + push_right) - 0.5 * wave_speed * (held_right * speed_right - held_left * speed_left)
    tangent_flux = 0.5 * (held_left * speed_left * drift_left + held_right * speed_right * drift_right) - 0.5 * wave_speed * (held_right * drift_right - held_left * drift_left)
    source_left = 0.5 * gravity_accel * (depth_left * depth_left - held_left * held_left)
    source_right = 0.5 * gravity_accel * (depth_right * depth_right - held_right * held_right)
    return (mass_flux, normal_flux, tangent_flux, source_left, source_right)

def advance(fields, roughness, ghosts):
    west_side, east_side, north_side, south_side = (ghosts[0], ghosts[1], ghosts[2], ghosts[3])

    def across(field_index):
        return jnp.concatenate([west_side[field_index][:, :, None], fields[field_index], east_side[field_index][:, :, None]], axis=2)

    def upward(field_index):
        return jnp.concatenate([north_side[field_index][:, None, :], fields[field_index], south_side[field_index][:, None, :]], axis=1)
    depth_x, along_x, cross_x, level_x = (across(0), across(1), across(2), across(3))
    east_terms = face_flux(depth_x[:, :, :-1], along_x[:, :, :-1], cross_x[:, :, :-1], level_x[:, :, :-1], depth_x[:, :, 1:], along_x[:, :, 1:], cross_x[:, :, 1:], level_x[:, :, 1:])
    depth_y, along_y, cross_y, level_y = (upward(0), upward(1), upward(2), upward(3))
    north_terms = face_flux(depth_y[:, :-1], cross_y[:, :-1], along_y[:, :-1], level_y[:, :-1], depth_y[:, 1:], cross_y[:, 1:], along_y[:, 1:], level_y[:, 1:])
    change_depth = east_terms[0][:, :, 1:] - east_terms[0][:, :, :-1] + (north_terms[0][:, 1:] - north_terms[0][:, :-1])
    change_along = east_terms[1][:, :, 1:] + east_terms[3][:, :, 1:] - (east_terms[1][:, :, :-1] + east_terms[4][:, :, :-1]) + (north_terms[2][:, 1:] - north_terms[2][:, :-1])
    change_cross = east_terms[2][:, :, 1:] - east_terms[2][:, :, :-1] + (north_terms[1][:, 1:] + north_terms[3][:, 1:] - (north_terms[1][:, :-1] + north_terms[4][:, :-1]))
    step_ratio = time_step / cell_width
    depth_new = fields[0] - step_ratio * change_depth
    along_new = fields[1] - step_ratio * change_along
    cross_new = fields[2] - step_ratio * change_cross
    flow_speed = jnp.sqrt(along_new * along_new + cross_new * cross_new) / depth_new
    damping = 1.0 + time_step * gravity_accel * roughness * roughness * flow_speed / jnp.power(depth_new, 4.0 / 3.0)
    return (depth_new, along_new / damping, cross_new / damping)

def face_strips(fields):
    return jnp.stack([fields[:, :, :, 0], fields[:, :, :, -1], fields[:, :, 0, :], fields[:, :, -1, :]])

def reference(state, terrain_local, terrain_store, wet_count, face_links, new_source, store_target):
    column_size = N_SUB * N_LANE
    device_total = N_TILE * column_size
    tile_total = device_total * SLOTS
    tile_ids = jnp.arange(tile_total, dtype=jnp.int32)
    device_ids = tile_ids // SLOTS
    band_ids = device_ids // column_size
    owner_device = jnp.maximum(new_source, 0) * column_size + device_ids % column_size
    targets = store_target.reshape(device_total, N_TILE)[owner_device]
    block_ids = jnp.argmax((targets == band_ids[:, None]).astype(jnp.int32), axis=1).astype(jnp.int32)
    fetched = terrain_store[:, owner_device * N_TILE + block_ids]
    terrain = jnp.where((new_source >= 0)[None, :, None, None], fetched, terrain_local).astype(jnp.float32)
    bed_level, roughness = (terrain[0], terrain[1])
    live_tile = tile_ids % SLOTS < wet_count[device_ids]
    link_device = face_links[:, 0, :]
    link_slot = face_links[:, 1, :]
    linked = link_device >= 0
    partner = jnp.maximum(link_device * SLOTS + link_slot, 0).astype(jnp.int32)
    depth_now, flow_x, flow_y = (state[0], state[1], state[2])
    for step_index in range(STEPS):
        fields = jnp.stack([depth_now, flow_x, flow_y, bed_level])
        own_strips = face_strips(fields)
        ghost_list = []
        for face_index in range(4):
            remote = own_strips[opposite_face[face_index]][:, partner[:, face_index]]
            mirrored = own_strips[face_index] * jnp.asarray(mirror_signs[face_index], jnp.float32)[:, None, None]
            ghost_list.append(jnp.where(linked[:, face_index][None, :, None], remote, mirrored))
        ghosts = jnp.stack(ghost_list)

        def one_device(device_index):
            start = (device_index * SLOTS).astype(jnp.int32)
            piece = lax.dynamic_slice_in_dim(fields, start, SLOTS, 1)
            rough_piece = lax.dynamic_slice_in_dim(roughness, start, SLOTS, 0)
            ghost_piece = lax.dynamic_slice_in_dim(ghosts, start, SLOTS, 2)
            return jnp.stack(advance(piece, rough_piece, ghost_piece))
        stacked = lax.map(one_device, jnp.arange(device_total, dtype=jnp.int32))
        updated = jnp.transpose(stacked, (1, 0, 2, 3, 4)).reshape(3, tile_total, TS, TS)
        depth_now, flow_x, flow_y = (updated[0], updated[1], updated[2])
    result = jnp.stack([depth_now, flow_x, flow_y])
    return jnp.where(live_tile[None, :, None, None], result, 0.0)
```

```python
import functools

import jax
import jax.numpy as jnp
from jax import lax
from jax.experimental import pallas as pl
from jax.experimental.pallas import tpu as pltpu
from jax.sharding import PartitionSpec as P

STEPS = 3
GRAVITY = 9.81
CELL = 30.0
DT = 1.0
ROWS = 32
AXES = ("region", "tile", "sub", "lane")
MESH = pl.DeviceIdType.MESH


def root(x):
    return x * lax.rsqrt(jnp.maximum(x, 1.2e-38))


def face_flux(eta_l, z_l, n_l, t_l, eta_r, z_r, n_r, t_r):
    z_face = jnp.maximum(z_l, z_r)
    h_l = jnp.maximum(eta_l - z_face, 0.0)
    h_r = jnp.maximum(eta_r - z_face, 0.0)
    wave = jnp.maximum(
        jnp.abs(n_l) + root(GRAVITY * h_l), jnp.abs(n_r) + root(GRAVITY * h_r)
    )
    m_l = h_l * n_l
    m_r = h_r * n_r
    d = h_r - h_l
    mass = (m_l + m_r) - wave * d
    base = (m_l * n_l + m_r * n_r) - wave * (m_r - m_l)
    press = (0.5 * GRAVITY) * d * (h_r + h_l)
    tang = (m_l * t_l + m_r * t_r) - wave * (h_r * t_r - h_l * t_l)
    return mass, base, press, tang


def kernel(
    sizes,
    wet_ref,
    links_ref,
    source_ref,
    target_ref,
    state_ref,
    local_ref,
    store_ref,
    out_ref,
    out_bed,
    out_rough,
    in_bed,
    in_rough,
    bed,
    drag,
    fields,
    prim,
    faces,
    tend,
    columns,
    rim,
    rim_t,
    own,
    ghost,
    msgs,
    strips_x,
    strips_n,
    strips_s,
    terrain_send,
    terrain_recv,
    strip_send,
    strip_recv,
):
    bands, subs, lanes, slots, size = sizes
    peers = subs * lanes
    band = lax.axis_index("tile")
    peer = lax.axis_index("sub") * lanes + lax.axis_index("lane")
    has_north = band > 0
    has_south = band < bands - 1

    def place(to_band, to_peer):
        return {"tile": to_band, "sub": to_peer // lanes, "lane": to_peer % lanes}

    barrier = pltpu.get_barrier_semaphore()

    def greet(to_band, to_peer):
        pl.semaphore_signal(
            barrier, inc=1, device_id=place(to_band, to_peer), device_id_type=MESH
        )

    for offset in range(1, peers):
        greet(band, lax.rem(peer + offset, peers))
    for offset in range(1, bands):
        greet(lax.rem(band + offset, bands), peer)

    @pl.when(has_north)
    def _():
        for offset in range(1, peers):
            greet(band - 1, lax.rem(peer + offset, peers))

    @pl.when(has_south)
    def _():
        for offset in range(1, peers):
            greet(band + 1, lax.rem(peer + offset, peers))

    for r in range(bands):
        block = jnp.int32(0)
        for j in range(bands):
            block = jnp.where(target_ref[j] == r, j, block)
        out_bed[r] = store_ref[0, block]
        out_rough[r] = store_ref[1, block]
    in_bed[band] = out_bed[band]
    in_rough[band] = out_rough[band]

    count = (peers - 1) + (bands - 1)
    count = count + jnp.where(has_north, peers - 1, 0) + jnp.where(has_south, peers - 1, 0)
    pl.semaphore_wait(barrier, count)

    for part, (source, target) in enumerate(((out_bed, in_bed), (out_rough, in_rough))):
        for offset in range(1, bands):
            to_band = lax.rem(band + offset, bands)
            pltpu.make_async_remote_copy(
                src_ref=source.at[to_band],
                dst_ref=target.at[band],
                send_sem=terrain_send.at[part],
                recv_sem=terrain_recv.at[part],
                device_id=place(to_band, peer),
                device_id_type=MESH,
            ).start()

    def wait_for(ref, length, sem):
        view = ref.at[pl.ds(0, length)]
        pltpu.make_async_copy(view, view, sem).wait()

    chunks = size // ROWS
    lane_id = lax.broadcasted_iota(jnp.int32, (ROWS, size), 1)

    def edge_columns(t, rows, q, value, before):
        rolled = pltpu.roll(value, 1 + 2 * q, axis=1)
        return jnp.where(lane_id // 2 == q, rolled, before)

    for q in range(3):
        for t in range(slots):
            prim[q, t, pl.ds(size, 8)] = jnp.zeros((8, size), jnp.float32)
    for t in range(slots):
        bed[t, pl.ds(size, 8)] = jnp.zeros((8, size), jnp.float32)
        rim[t] = jnp.zeros((size, size), jnp.float32)

    wait_for(in_bed, bands - 1, terrain_recv.at[0])

    for t in range(slots):
        fetched = in_bed[jnp.maximum(source_ref[t], 0)].astype(jnp.float32)
        bed[t, pl.ds(0, size)] = jnp.where(
            source_ref[t] >= 0, fetched, local_ref[0, t].astype(jnp.float32)
        )

    def first(i, carry):
        t = i // chunks
        rows = pl.ds(pl.multiple_of((i % chunks) * ROWS, ROWS), ROWS)
        h = state_ref[0, t, rows]
        z = bed[t, rows]
        inv = 1.0 / h
        u = state_ref[1, t, rows] * inv
        v = state_ref[2, t, rows] * inv
        prim[0, t, rows] = h + z
        prim[1, t, rows] = u
        prim[2, t, rows] = v
        value = edge_columns(t, rows, 0, h, jnp.zeros_like(h))
        value = edge_columns(t, rows, 1, u, value)
        value = edge_columns(t, rows, 2, v, value)
        columns[t, rows] = edge_columns(t, rows, 3, z, value)
        return carry

    lax.fori_loop(0, slots * chunks, first, 0)

    def send_strips(step):
        current = state_ref if step == 0 else fields
        for t in range(slots):
            turned = jnp.transpose(columns[t])
            for q in range(4):
                if q == 3 and step > 0:
                    for f in range(4):
                        msgs[step, f, pl.ds(4 * t + 3, 1)] = own[3, pl.ds(f * slots + t, 1)]
                    continue
                if q == 0:
                    top, low = current[0, t, pl.ds(0, 1)], current[0, t, pl.ds(size - 1, 1)]
                elif q == 3:
                    top, low = bed[t, pl.ds(0, 1)], bed[t, pl.ds(size - 1, 1)]
                else:
                    top, low = prim[q, t, pl.ds(0, 1)], prim[q, t, pl.ds(size - 1, 1)]
                strip = (turned[2 * q + 1 : 2 * q + 2], turned[2 * q : 2 * q + 1], top, low)
                for f in range(4):
                    msgs[step, f, pl.ds(4 * t + q, 1)] = strip[f]
                    own[q, pl.ds(f * slots + t, 1)] = strip[f]
        strips_x[step][peer] = msgs[step, pl.ds(0, 2)]

        def send(kind, source, target, to_band, to_peer):
            pltpu.make_async_remote_copy(
                src_ref=source,
                dst_ref=target.at[peer],
                send_sem=strip_send.at[step, kind],
                recv_sem=strip_recv.at[step, kind],
                device_id=place(to_band, to_peer),
                device_id_type=MESH,
            ).start()

        @pl.when(has_south)
        def _():
            for offset in range(peers):
                to_peer = lax.rem(peer + offset, peers)
                send(1, msgs.at[step, 3], strips_n[step], band + 1, to_peer)

        @pl.when(has_north)
        def _():
            for offset in range(peers):
                to_peer = lax.rem(peer + offset, peers)
                send(2, msgs.at[step, 2], strips_s[step], band - 1, to_peer)

        for offset in range(1, peers):
            to_peer = lax.rem(peer + offset, peers)
            send(0, msgs.at[step, pl.ds(0, 2)], strips_x[step], band, to_peer)

    def inner(i, carry):
        t = i // chunks
        start = pl.multiple_of((i % chunks) * ROWS, ROWS)
        rows = pl.ds(start, ROWS)
        below = pl.ds(start + 1, ROWS)
        eta, u, v, z = prim[0, t, rows], prim[1, t, rows], prim[2, t, rows], bed[t, rows]
        east = [pltpu.roll(x, size - 1, axis=1) for x in (eta, z, u, v)]
        mass, base, press, tang = face_flux(eta, z, u, v, *east)
        inside = lane_id < size - 1
        mass = jnp.where(inside, mass, 0.0)
        far = jnp.where(inside, base + press, 0.0)
        near = jnp.where(inside, base - press, 0.0)
        tang = jnp.where(inside, tang, 0.0)
        tend[0, t, rows] = mass - pltpu.roll(mass, 1, axis=1)
        tend[1, t, rows] = far - pltpu.roll(near, 1, axis=1)
        tend[2, t, rows] = tang - pltpu.roll(tang, 1, axis=1)
        mass, base, press, tang = face_flux(
            eta, z, v, u, prim[0, t, below], bed[t, below], prim[2, t, below], prim[1, t, below]
        )
        into = pl.ds(pl.multiple_of(start + 8, 8), ROWS)
        faces[0, t, into] = mass
        faces[1, t, into] = base + press
        faces[2, t, into] = base - press
        faces[3, t, into] = tang
        return carry

    def wait_strips(step):
        if peers > 1:
            wait_for(strips_x[step], peers - 1, strip_recv.at[step, 0])

        @pl.when(has_north)
        def _():
            wait_for(strips_n[step], peers, strip_recv.at[step, 1])

        @pl.when(has_south)
        def _():
            wait_for(strips_s[step], peers, strip_recv.at[step, 2])

    def rims(step):
        for t in range(slots):
            for f in range(4):
                device = links_ref[t, 0, f]
                linked = device >= 0
                who = lax.rem(jnp.maximum(device, 0), peers)
                rows = pl.ds(4 * jnp.maximum(links_ref[t, 1, f], 0), 4)
                if f < 2:
                    remote = strips_x[step][who, 1 - f, rows]
                else:
                    remote = (strips_n if f == 2 else strips_s)[step][who, rows]
                row = pl.ds(f * slots + t, 1)
                for q in range(4):
                    mine = own[q, row]
                    if q == (1 if f < 2 else 2):
                        mine = -mine
                    ghost[q, row] = jnp.where(linked, remote[q : q + 1], mine)
        row_id = lax.broadcasted_iota(jnp.int32, (4 * slots, size), 0) // slots
        near_side = row_id % 2 == 0
        across = row_id < 2
        g = [ghost[q] for q in range(4)]
        o = [own[q] for q in range(4)]

        def ordered(x):
            h, u, v, z = x
            return h + z, z, jnp.where(across, u, v), jnp.where(across, v, u)

        go, oo = ordered(g), ordered(o)
        left = [jnp.where(near_side, a, b) for a, b in zip(go, oo)]
        right = [jnp.where(near_side, b, a) for a, b in zip(go, oo)]
        mass, base, press, tang = face_flux(*left, *right)
        normal = jnp.where(near_side, base - press, base + press)

        def pick(value, f, t):
            return value[f * slots + t : f * slots + t + 1]

        for t in range(slots):
            for q, value in enumerate((mass, normal, tang)):
                rim[t, pl.ds(2 * q, 1)] = pick(value, 1, t)
                rim[t, pl.ds(2 * q + 1, 1)] = -pick(value, 0, t)
            top, low = pl.ds(7, 1), pl.ds(7 + size, 1)
            faces[0, t, top] = pick(mass, 2, t)
            faces[2, t, top] = pick(normal, 2, t)
            faces[3, t, top] = pick(tang, 2, t)
            faces[0, t, low] = pick(mass, 3, t)
            faces[1, t, low] = pick(normal, 3, t)
            faces[3, t, low] = pick(tang, 3, t)
            rim_t[t] = jnp.transpose(rim[t])

    def update(step, i, carry):
        last = step == STEPS - 1
        current = state_ref if step == 0 else fields
        t = i // chunks
        start = pl.multiple_of((i % chunks) * ROWS, ROWS)
        rows = pl.ds(start, ROWS)
        here = pl.ds(pl.multiple_of(start + 8, 8), ROWS)
        above = pl.ds(start + 7, ROWS)
        turned = rim_t[t, rows]
        border = (lane_id == 0) | (lane_id == size - 1)

        def sides(q):
            return jnp.where(border, pltpu.roll(turned, size - 1 - 2 * q, axis=1), 0.0)

        ratio = 0.5 * DT / CELL
        h = current[0, t, rows] - ratio * (
            tend[0, t, rows] + sides(0) + (faces[0, t, here] - faces[0, t, above])
        )
        qx = current[1, t, rows] - ratio * (
            tend[1, t, rows] + sides(1) + (faces[3, t, here] - faces[3, t, above])
        )
        qy = current[2, t, rows] - ratio * (
            tend[2, t, rows] + sides(2) + (faces[1, t, here] - faces[2, t, above])
        )
        power = jnp.exp((-7.0 / 3.0) * jnp.log(h))
        damp = 1.0 / (1.0 + drag[t, rows] * root(qx * qx + qy * qy) * power)
        qx = qx * damp
        qy = qy * damp
        if last:
            live = t < wet_ref[0]
            out_ref[0, t, rows] = jnp.where(live, h, 0.0)
            out_ref[1, t, rows] = jnp.where(live, qx, 0.0)
            out_ref[2, t, rows] = jnp.where(live, qy, 0.0)
        else:
            fields[0, t, rows] = h
            fields[1, t, rows] = qx
            fields[2, t, rows] = qy
            inv = 1.0 / h
            u = qx * inv
            v = qy * inv
            prim[0, t, rows] = h + bed[t, rows]
            prim[1, t, rows] = u
            prim[2, t, rows] = v
            value = edge_columns(t, rows, 0, h, jnp.zeros_like(h))
            value = edge_columns(t, rows, 1, u, value)
            columns[t, rows] = edge_columns(t, rows, 2, v, value)
        return carry

    for step in range(STEPS):
        send_strips(step)
        lax.fori_loop(0, slots * chunks, inner, 0)
        if step == 0:
            wait_for(in_rough, bands - 1, terrain_recv.at[1])
            for t in range(slots):
                fetched = in_rough[jnp.maximum(source_ref[t], 0)].astype(jnp.float32)
                rough = jnp.where(
                    source_ref[t] >= 0, fetched, local_ref[1, t].astype(jnp.float32)
                )
                drag[t] = (DT * GRAVITY) * rough * rough
        wait_strips(step)
        rims(step)
        lax.fori_loop(0, slots * chunks, functools.partial(update, step), 0)

    for part, source in enumerate((out_bed, out_rough)):
        wait_for(source, bands - 1, terrain_send.at[part])
    for step in range(STEPS):
        wait_for(strips_x[step], peers - 1, strip_send.at[step, 0])

        @pl.when(has_south)
        def _():
            wait_for(strips_n[step], peers, strip_send.at[step, 1])

        @pl.when(has_north)
        def _():
            wait_for(strips_s[step], peers, strip_send.at[step, 2])


def local(sizes, state, terrain_local, terrain_store, wet_count, face_links, new_source, store_target):
    bands, subs, lanes, slots, size = sizes
    peers = subs * lanes
    f32, bf16 = jnp.float32, jnp.bfloat16
    block = (bands, size, size)
    smem = pl.BlockSpec(memory_space=pltpu.SMEM)
    vmem = pl.BlockSpec(memory_space=pltpu.VMEM)
    msg = (4 * slots, size)
    return pl.pallas_call(
        functools.partial(kernel, sizes),
        out_shape=jax.ShapeDtypeStruct(state.shape, f32),
        in_specs=[smem] * 4 + [vmem] * 3,
        out_specs=vmem,
        scratch_shapes=[
            pltpu.VMEM(block, bf16),
            pltpu.VMEM(block, bf16),
            pltpu.VMEM(block, bf16),
            pltpu.VMEM(block, bf16),
            pltpu.VMEM((slots, size + 8, size), f32),
            pltpu.VMEM((slots, size, size), f32),
            pltpu.VMEM((3, slots, size, size), f32),
            pltpu.VMEM((3, slots, size + 8, size), f32),
            pltpu.VMEM((4, slots, size + 16, size), f32),
            pltpu.VMEM((3, slots, size, size), f32),
            pltpu.VMEM((slots, size, size), f32),
            pltpu.VMEM((slots, size, size), f32),
            pltpu.VMEM((slots, size, size), f32),
            pltpu.VMEM((4,) + msg, f32),
            pltpu.VMEM((4,) + msg, f32),
            pltpu.VMEM((STEPS, 4) + msg, f32),
            [pltpu.VMEM((peers, 2) + msg, f32) for _ in range(STEPS)],
            [pltpu.VMEM((peers,) + msg, f32) for _ in range(STEPS)],
            [pltpu.VMEM((peers,) + msg, f32) for _ in range(STEPS)],
            pltpu.SemaphoreType.DMA((2,)),
            pltpu.SemaphoreType.DMA((2,)),
            pltpu.SemaphoreType.DMA((STEPS, 3)),
            pltpu.SemaphoreType.DMA((STEPS, 3)),
        ],
        compiler_params=pltpu.CompilerParams(
            collective_id=0, has_side_effects=True, vmem_limit_bytes=32 * 1024 * 1024
        ),
    )(wet_count, face_links, new_source, store_target, state, terrain_local, terrain_store)


def solution(mesh):
    shape = mesh.shape
    devices = P(None, AXES, None, None)
    flat = P(AXES)

    def whole(state, *rest):
        def part(block, *others):
            sizes = (shape["tile"], shape["sub"], shape["lane"], block.shape[1], block.shape[2])
            return local(sizes, block, *others)

        return jax.shard_map(
            part,
            mesh=mesh,
            in_specs=(devices, devices, devices, flat, P(AXES, None, None), flat, flat),
            out_specs=devices,
            check_vma=False,
        )(state, *rest)

    return whole
```

```python
import functools

import jax
import jax.numpy as jnp
from jax import lax
from jax.experimental import pallas as pl
from jax.experimental.pallas import tpu as pltpu
from jax.sharding import PartitionSpec as P

STEPS = 3
GRAVITY = 9.81
CELL = 30.0
DT = 1.0
ROWS = 128
AXES = ("region", "tile", "sub", "lane")
MESH = pl.DeviceIdType.MESH


def root(x):
    return x * lax.rsqrt(jnp.maximum(x, 1.2e-38))


def face_flux(eta_l, z_l, n_l, t_l, eta_r, z_r, n_r, t_r):
    z_face = jnp.maximum(z_l, z_r)
    h_l = jnp.maximum(eta_l - z_face, 0.0)
    h_r = jnp.maximum(eta_r - z_face, 0.0)
    wave = jnp.maximum(
        jnp.abs(n_l) + root(GRAVITY * h_l), jnp.abs(n_r) + root(GRAVITY * h_r)
    )
    m_l = h_l * n_l
    m_r = h_r * n_r
    d = h_r - h_l
    mass = (m_l + m_r) - wave * d
    base = (m_l * n_l + m_r * n_r) - wave * (m_r - m_l)
    press = (0.5 * GRAVITY) * d * (h_r + h_l)
    tang = (m_l * t_l + m_r * t_r) - wave * (h_r * t_r - h_l * t_l)
    return mass, base, press, tang


def kernel(
    sizes,
    wet_hbm,
    links_hbm,
    source_hbm,
    target_hbm,
    state_hbm,
    local_hbm,
    store_hbm,
    out_ref,
    wet_ref,
    links_ref,
    source_ref,
    target_ref,
    state_ref,
    local_ref,
    store_ref,
    out_bed,
    out_rough,
    in_bed,
    in_rough,
    bed,
    drag,
    fields,
    prim,
    faces,
    tend,
    columns,
    rim,
    rim_t,
    own,
    ghost,
    msgs,
    strips_x,
    strips_n,
    strips_s,
    edge_msgs,
    edge_in,
    load_sem,
    terrain_send,
    terrain_recv,
    strip_send,
    strip_recv,
):
    bands, subs, lanes, slots, size = sizes
    peers = subs * lanes
    total = bands * peers
    band = lax.axis_index("tile")
    peer = lax.axis_index("sub") * lanes + lax.axis_index("lane")
    me = band * peers + peer
    has_north = band > 0
    has_south = band < bands - 1

    loads = [
        pltpu.make_async_copy(source, target, load_sem.at[i])
        for i, (source, target) in enumerate(
            (
                (target_hbm, target_ref),
                (store_hbm, store_ref),
                (source_hbm, source_ref),
                (state_hbm, state_ref),
                (local_hbm, local_ref),
                (links_hbm, links_ref),
                (wet_hbm, wet_ref),
            )
        )
    ]
    for load in loads:
        load.start()

    def place(to_band, to_peer):
        return {"tile": to_band, "sub": to_peer // lanes, "lane": to_peer % lanes}

    def each_other(body):
        def one(offset, carry):
            other = lax.rem(me + offset, total)
            body(other // peers, other % peers)
            return carry

        lax.fori_loop(1, total, one, 0, unroll=total <= 16)

    barrier = pltpu.get_barrier_semaphore()

    def greet(to_band, to_peer):
        pl.semaphore_signal(
            barrier, inc=1, device_id=place(to_band, to_peer), device_id_type=MESH
        )

    each_other(greet)

    def wait_for(ref, length, sem):
        view = ref.at[pl.ds(0, length)]
        pltpu.make_async_copy(view, view, sem).wait()

    wide_id = lax.broadcasted_iota(jnp.int32, (size, size), 1)

    for q in range(3):
        for t in range(slots):
            prim[q, t, pl.ds(size, 8)] = jnp.zeros((8, size), jnp.float32)
    for t in range(slots):
        bed[t, pl.ds(size, 8)] = jnp.zeros((8, size), jnp.float32)
        rim[t] = jnp.zeros((size, size), jnp.float32)
    msgs[...] = jnp.zeros_like(msgs)
    edge_msgs[...] = jnp.zeros_like(edge_msgs)

    loads[0].wait()
    loads[1].wait()
    sides = jnp.zeros((size, size), jnp.float32)
    for r in range(bands):
        block = jnp.int32(0)
        for j in range(bands):
            block = jnp.where(target_ref[j] == r, j, block)
        level = store_ref[0, block]
        out_bed[r] = level
        out_rough[r] = store_ref[1, block]
        level = level.astype(jnp.float32)
        sides = jnp.where(wide_id // 2 == r, pltpu.roll(level, 1 + 2 * r, axis=1), sides)
        if r > 0:
            edge_msgs[r - 1, pl.ds(2, 1)] = level[0:1]
        if r < bands - 1:
            edge_msgs[r + 1, pl.ds(3, 1)] = level[size - 1 : size]
    sides = jnp.transpose(sides)
    loads[2].wait()
    for r in range(bands):
        edge_msgs[r, pl.ds(0, 1)] = sides[2 * r + 1 : 2 * r + 2]
        edge_msgs[r, pl.ds(1, 1)] = sides[2 * r : 2 * r + 1]
        for t in range(slots):
            row = jnp.full((1, size), source_ref[t].astype(jnp.float32))
            edge_msgs[r, pl.ds(4 + t, 1)] = row
    in_bed[band] = out_bed[band]
    in_rough[band] = out_rough[band]
    edge_in[me] = edge_msgs[band]
    for load in loads[3:]:
        load.wait()

    chunks = size // ROWS
    lane_id = lax.broadcasted_iota(jnp.int32, (ROWS, size), 1)

    def edge_columns(t, rows, q, value, before):
        rolled = pltpu.roll(value, 1 + 2 * q, axis=1)
        return jnp.where(lane_id // 2 == q, rolled, before)

    def first(i, carry):
        t = i // chunks
        rows = pl.ds(pl.multiple_of((i % chunks) * ROWS, ROWS), ROWS)
        h = state_ref[0, t, rows]
        inv = 1.0 / h
        u = state_ref[1, t, rows] * inv
        v = state_ref[2, t, rows] * inv
        prim[1, t, rows] = u
        prim[2, t, rows] = v
        value = edge_columns(t, rows, 0, h, jnp.zeros_like(h))
        value = edge_columns(t, rows, 1, u, value)
        value = edge_columns(t, rows, 2, v, value)
        z = local_ref[0, t, rows].astype(jnp.float32)
        columns[t, rows] = edge_columns(t, rows, 3, z, value)
        return carry

    lax.fori_loop(0, slots * chunks, first, 0)

    def send_strips(step):
        current = state_ref if step == 0 else fields
        for t in range(slots):
            turned = jnp.transpose(columns[t])
            for q in range(4):
                if q == 3 and step > 0:
                    continue
                if q == 0:
                    top, low = current[0, t, pl.ds(0, 1)], current[0, t, pl.ds(size - 1, 1)]
                elif q == 3:
                    level = local_ref[0, t].astype(jnp.float32)
                    top, low = level[0:1], level[size - 1 : size]
                else:
                    top, low = prim[q, t, pl.ds(0, 1)], prim[q, t, pl.ds(size - 1, 1)]
                strip = (turned[2 * q + 1 : 2 * q + 2], turned[2 * q : 2 * q + 1], top, low)
                for f in range(4):
                    msgs[step, f, pl.ds(4 * t + q, 1)] = strip[f]
                    own[q, pl.ds(f * slots + t, 1)] = strip[f]
        strips_x[step][peer] = msgs[step, pl.ds(0, 2)]
        if step == 0:
            pl.semaphore_wait(barrier, total - 1)

        def send(kind, source, target, to_band, to_peer):
            pltpu.make_async_remote_copy(
                src_ref=source,
                dst_ref=target.at[peer],
                send_sem=strip_send.at[step, kind],
                recv_sem=strip_recv.at[step, kind],
                device_id=place(to_band, to_peer),
                device_id_type=MESH,
            ).start()

        @pl.when(has_south)
        def _():
            for offset in range(peers):
                to_peer = lax.rem(peer + offset, peers)
                send(1, msgs.at[step, 3], strips_n[step], band + 1, to_peer)

        @pl.when(has_north)
        def _():
            for offset in range(peers):
                to_peer = lax.rem(peer + offset, peers)
                send(2, msgs.at[step, 2], strips_s[step], band - 1, to_peer)

        for offset in range(1, peers):
            to_peer = lax.rem(peer + offset, peers)
            send(0, msgs.at[step, pl.ds(0, 2)], strips_x[step], band, to_peer)

    def inner(i, carry):
        t = i // chunks
        start = pl.multiple_of((i % chunks) * ROWS, ROWS)
        rows = pl.ds(start, ROWS)
        below = pl.ds(start + 1, ROWS)
        eta, u, v, z = prim[0, t, rows], prim[1, t, rows], prim[2, t, rows], bed[t, rows]
        east = [pltpu.roll(x, size - 1, axis=1) for x in (eta, z, u, v)]
        mass, base, press, tang = face_flux(eta, z, u, v, *east)
        inside = lane_id < size - 1
        mass = jnp.where(inside, mass, 0.0)
        far = jnp.where(inside, base + press, 0.0)
        near = jnp.where(inside, base - press, 0.0)
        tang = jnp.where(inside, tang, 0.0)
        tend[0, t, rows] = mass - pltpu.roll(mass, 1, axis=1)
        tend[1, t, rows] = far - pltpu.roll(near, 1, axis=1)
        tend[2, t, rows] = tang - pltpu.roll(tang, 1, axis=1)
        mass, base, press, tang = face_flux(
            eta, z, v, u, prim[0, t, below], bed[t, below], prim[2, t, below], prim[1, t, below]
        )
        into = pl.ds(pl.multiple_of(start + 8, 8), ROWS)
        faces[0, t, into] = mass
        faces[1, t, into] = base + press
        faces[2, t, into] = base - press
        faces[3, t, into] = tang
        return carry

    def wait_strips(step):
        if peers > 1:
            wait_for(strips_x[step], peers - 1, strip_recv.at[step, 0])

        @pl.when(has_north)
        def _():
            wait_for(strips_n[step], peers, strip_recv.at[step, 1])

        @pl.when(has_south)
        def _():
            wait_for(strips_s[step], peers, strip_recv.at[step, 2])

    def rims(step):
        for t in range(slots):
            for f in range(4):
                device = links_ref[t, 0, f]
                linked = device >= 0
                who = lax.rem(jnp.maximum(device, 0), peers)
                slot = jnp.maximum(links_ref[t, 1, f], 0)
                rows = pl.ds(4 * slot, 4)
                if f < 2:
                    remote = strips_x[step][who, 1 - f, rows]
                else:
                    remote = (strips_n if f == 2 else strips_s)[step][who, rows]
                row = pl.ds(f * slots + t, 1)
                if step == 0:
                    at = band + (0, 0, -1, 1)[f]
                    holder = edge_in[jnp.clip(at, 0, bands - 1) * peers + who, pl.ds(4 + slot, 1)]
                    level = remote[3:4]
                    for r in range(bands):
                        edge = edge_in[r * peers + who, pl.ds((1, 0, 3, 2)[f], 1)]
                        level = jnp.where(holder == float(r), edge, level)
                    ghost[3, row] = jnp.where(linked, level, own[3, row])
                for q in range(3):
                    mine = own[q, row]
                    if q == (1 if f < 2 else 2):
                        mine = -mine
                    ghost[q, row] = jnp.where(linked, remote[q : q + 1], mine)
        row_id = lax.broadcasted_iota(jnp.int32, (4 * slots, size), 0) // slots
        near_side = row_id % 2 == 0
        across = row_id < 2
        g = [ghost[q] for q in range(4)]
        o = [own[q] for q in range(4)]

        def ordered(x):
            h, u, v, z = x
            return h + z, z, jnp.where(across, u, v), jnp.where(across, v, u)

        go, oo = ordered(g), ordered(o)
        left = [jnp.where(near_side, a, b) for a, b in zip(go, oo)]
        right = [jnp.where(near_side, b, a) for a, b in zip(go, oo)]
        mass, base, press, tang = face_flux(*left, *right)
        normal = jnp.where(near_side, base - press, base + press)

        def pick(value, f, t):
            return value[f * slots + t : f * slots + t + 1]

        for t in range(slots):
            for q, value in enumerate((mass, normal, tang)):
                rim[t, pl.ds(2 * q, 1)] = pick(value, 1, t)
                rim[t, pl.ds(2 * q + 1, 1)] = -pick(value, 0, t)
            top, low = pl.ds(7, 1), pl.ds(7 + size, 1)
            faces[0, t, top] = pick(mass, 2, t)
            faces[2, t, top] = pick(normal, 2, t)
            faces[3, t, top] = pick(tang, 2, t)
            faces[0, t, low] = pick(mass, 3, t)
            faces[1, t, low] = pick(normal, 3, t)
            faces[3, t, low] = pick(tang, 3, t)
            rim_t[t] = jnp.transpose(rim[t])

    def update(step, i, carry):
        last = step == STEPS - 1
        current = state_ref if step == 0 else fields
        t = i // chunks
        start = pl.multiple_of((i % chunks) * ROWS, ROWS)
        rows = pl.ds(start, ROWS)
        here = pl.ds(pl.multiple_of(start + 8, 8), ROWS)
        above = pl.ds(start + 7, ROWS)
        turned = rim_t[t, rows]
        border = (lane_id == 0) | (lane_id == size - 1)

        def sides(q):
            return jnp.where(border, pltpu.roll(turned, size - 1 - 2 * q, axis=1), 0.0)

        ratio = 0.5 * DT / CELL
        h = current[0, t, rows] - ratio * (
            tend[0, t, rows] + sides(0) + (faces[0, t, here] - faces[0, t, above])
        )
        qx = current[1, t, rows] - ratio * (
            tend[1, t, rows] + sides(1) + (faces[3, t, here] - faces[3, t, above])
        )
        qy = current[2, t, rows] - ratio * (
            tend[2, t, rows] + sides(2) + (faces[1, t, here] - faces[2, t, above])
        )
        power = jnp.exp((-7.0 / 3.0) * jnp.log(h))
        damp = 1.0 / (1.0 + drag[t, rows] * root(qx * qx + qy * qy) * power)
        qx = qx * damp
        qy = qy * damp
        if last:
            live = t < wet_ref[0]
            out_ref[0, t, rows] = jnp.where(live, h, 0.0)
            out_ref[1, t, rows] = jnp.where(live, qx, 0.0)
            out_ref[2, t, rows] = jnp.where(live, qy, 0.0)
        else:
            fields[0, t, rows] = h
            fields[1, t, rows] = qx
            fields[2, t, rows] = qy
            inv = 1.0 / h
            u = qx * inv
            v = qy * inv
            prim[0, t, rows] = h + bed[t, rows]
            prim[1, t, rows] = u
            prim[2, t, rows] = v
            value = edge_columns(t, rows, 0, h, jnp.zeros_like(h))
            value = edge_columns(t, rows, 1, u, value)
            columns[t, rows] = edge_columns(t, rows, 2, v, value)
        return carry

    def send_terrain():
        def send_edges(to_band, to_peer):
            pltpu.make_async_remote_copy(
                src_ref=edge_msgs.at[to_band],
                dst_ref=edge_in.at[me],
                send_sem=terrain_send.at[2],
                recv_sem=terrain_recv.at[2],
                device_id=place(to_band, to_peer),
                device_id_type=MESH,
            ).start()

        each_other(send_edges)
        for part, (source, target) in enumerate(((out_bed, in_bed), (out_rough, in_rough))):
            for offset in range(1, bands):
                to_band = lax.rem(band + offset, bands)
                pltpu.make_async_remote_copy(
                    src_ref=source.at[to_band],
                    dst_ref=target.at[band],
                    send_sem=terrain_send.at[part],
                    recv_sem=terrain_recv.at[part],
                    device_id=place(to_band, peer),
                    device_id_type=MESH,
                ).start()

    def fill_bed():
        wait_for(in_bed, bands - 1, terrain_recv.at[0])
        for t in range(slots):
            fetched = in_bed[jnp.maximum(source_ref[t], 0)].astype(jnp.float32)
            level = jnp.where(source_ref[t] >= 0, fetched, local_ref[0, t].astype(jnp.float32))
            bed[t, pl.ds(0, size)] = level
            prim[0, t, pl.ds(0, size)] = level + state_ref[0, t]
            own[3, pl.ds(2 * slots + t, 1)] = level[0:1]
            own[3, pl.ds(3 * slots + t, 1)] = level[size - 1 : size]

    def own_edges():
        wait_for(edge_in, total - 1, terrain_recv.at[2])
        for t in range(slots):
            holder = jnp.maximum(source_ref[t], 0) * peers + peer
            for f in range(2):
                row = pl.ds(f * slots + t, 1)
                edge = edge_in[holder, pl.ds(f, 1)]
                own[3, row] = jnp.where(source_ref[t] >= 0, edge, own[3, row])

    def fill_drag():
        wait_for(in_rough, bands - 1, terrain_recv.at[1])
        for t in range(slots):
            fetched = in_rough[jnp.maximum(source_ref[t], 0)].astype(jnp.float32)
            rough = jnp.where(source_ref[t] >= 0, fetched, local_ref[1, t].astype(jnp.float32))
            drag[t] = (DT * GRAVITY) * rough * rough

    for step in range(STEPS):
        send_strips(step)
        if step == 0:
            send_terrain()
            fill_bed()
        lax.fori_loop(0, slots * chunks, inner, 0)
        wait_strips(step)
        if step == 0:
            own_edges()
        rims(step)
        if step == 0:
            fill_drag()
        lax.fori_loop(0, slots * chunks, functools.partial(update, step), 0)

    wait_for(edge_in, total - 1, terrain_send.at[2])
    for part, source in enumerate((out_bed, out_rough)):
        wait_for(source, bands - 1, terrain_send.at[part])
    for step in range(STEPS):
        wait_for(strips_x[step], peers - 1, strip_send.at[step, 0])

        @pl.when(has_south)
        def _():
            wait_for(strips_n[step], peers, strip_send.at[step, 1])

        @pl.when(has_north)
        def _():
            wait_for(strips_s[step], peers, strip_send.at[step, 2])


def local(sizes, state, terrain_local, terrain_store, wet_count, face_links, new_source, store_target):
    bands, subs, lanes, slots, size = sizes
    peers = subs * lanes
    f32, bf16 = jnp.float32, jnp.bfloat16
    block = (bands, size, size)
    hbm = pl.BlockSpec(memory_space=pl.ANY)
    vmem = pl.BlockSpec(memory_space=pltpu.VMEM)
    msg = (4 * slots, size)
    return pl.pallas_call(
        functools.partial(kernel, sizes),
        out_shape=jax.ShapeDtypeStruct(state.shape, f32),
        in_specs=[hbm] * 7,
        out_specs=vmem,
        scratch_shapes=[
            pltpu.SMEM(wet_count.shape, jnp.int32),
            pltpu.SMEM(face_links.shape, jnp.int32),
            pltpu.SMEM(new_source.shape, jnp.int32),
            pltpu.SMEM(store_target.shape, jnp.int32),
            pltpu.VMEM(state.shape, f32),
            pltpu.VMEM(terrain_local.shape, bf16),
            pltpu.VMEM(terrain_store.shape, bf16),
            pltpu.VMEM(block, bf16),
            pltpu.VMEM(block, bf16),
            pltpu.VMEM(block, bf16),
            pltpu.VMEM(block, bf16),
            pltpu.VMEM((slots, size + 8, size), f32),
            pltpu.VMEM((slots, size, size), f32),
            pltpu.VMEM((3, slots, size, size), f32),
            pltpu.VMEM((3, slots, size + 8, size), f32),
            pltpu.VMEM((4, slots, size + 16, size), f32),
            pltpu.VMEM((3, slots, size, size), f32),
            pltpu.VMEM((slots, size, size), f32),
            pltpu.VMEM((slots, size, size), f32),
            pltpu.VMEM((slots, size, size), f32),
            pltpu.VMEM((4,) + msg, f32),
            pltpu.VMEM((4,) + msg, f32),
            pltpu.VMEM((STEPS, 4) + msg, f32),
            [pltpu.VMEM((peers, 2) + msg, f32) for _ in range(STEPS)],
            [pltpu.VMEM((peers,) + msg, f32) for _ in range(STEPS)],
            [pltpu.VMEM((peers,) + msg, f32) for _ in range(STEPS)],
            pltpu.VMEM((bands, 8, size), f32),
            pltpu.VMEM((bands * peers, 8, size), f32),
            pltpu.SemaphoreType.DMA((7,)),
            pltpu.SemaphoreType.DMA((3,)),
            pltpu.SemaphoreType.DMA((3,)),
            pltpu.SemaphoreType.DMA((STEPS, 3)),
            pltpu.SemaphoreType.DMA((STEPS, 3)),
        ],
        compiler_params=pltpu.CompilerParams(
            collective_id=0, has_side_effects=True, vmem_limit_bytes=32 * 1024 * 1024
        ),
    )(wet_count, face_links, new_source, store_target, state, terrain_local, terrain_store)


def solution(mesh):
    shape = mesh.shape
    devices = P(None, AXES, None, None)
    flat = P(AXES)

    def whole(state, *rest):
        def part(block, *others):
            sizes = (shape["tile"], shape["sub"], shape["lane"], block.shape[1], block.shape[2])
            return local(sizes, block, *others)

        return jax.shard_map(
            part,
            mesh=mesh,
            in_specs=(devices, devices, devices, flat, P(AXES, None, None), flat, flat),
            out_specs=devices,
            check_vma=False,
        )(state, *rest)

    return whole
```

```python
import functools

import jax
import jax.numpy as jnp
from jax import lax
from jax.experimental import pallas as pl
from jax.experimental.pallas import tpu as pltpu
from jax.sharding import PartitionSpec as P

STEPS = 3
GRAVITY = 9.81
CELL = 30.0
DT = 1.0
ROWS = 128
CODE = 4096.0
AXES = ("region", "tile", "sub", "lane")
MESH = pl.DeviceIdType.MESH


def root(x):
    return x * lax.rsqrt(jnp.maximum(x, 1.2e-38))


def face_flux(eta_l, z_l, n_l, t_l, eta_r, z_r, n_r, t_r):
    z_face = jnp.maximum(z_l, z_r)
    h_l = jnp.maximum(eta_l - z_face, 0.0)
    h_r = jnp.maximum(eta_r - z_face, 0.0)
    wave = jnp.maximum(
        jnp.abs(n_l) + root(GRAVITY * h_l), jnp.abs(n_r) + root(GRAVITY * h_r)
    )
    m_l = h_l * n_l
    m_r = h_r * n_r
    d = h_r - h_l
    mass = (m_l + m_r) - wave * d
    base = (m_l * n_l + m_r * n_r) - wave * (m_r - m_l)
    press = (0.5 * GRAVITY) * d * (h_r + h_l)
    tang = (m_l * t_l + m_r * t_r) - wave * (h_r * t_r - h_l * t_l)
    return mass, base, press, tang


def kernel(
    sizes,
    wet_hbm,
    links_hbm,
    source_hbm,
    target_hbm,
    state_hbm,
    local_hbm,
    store_hbm,
    out_ref,
    wet_ref,
    links_ref,
    source_ref,
    target_ref,
    state_ref,
    local_ref,
    store_ref,
    out_bed,
    out_rough,
    in_bed,
    in_rough,
    bed,
    drag,
    fields,
    prim,
    faces,
    tend,
    columns,
    rim,
    rim_t,
    own,
    ghost,
    msgs,
    strips_x,
    strips_n,
    strips_s,
    edge_msgs,
    edge_in,
    load_sem,
    terrain_send,
    terrain_recv,
    strip_send,
    strip_recv,
):
    bands, subs, lanes, slots, size = sizes
    peers = subs * lanes
    total = bands * peers
    band = lax.axis_index("tile")
    peer = lax.axis_index("sub") * lanes + lax.axis_index("lane")
    me = band * peers + peer
    has_north = band > 0
    has_south = band < bands - 1

    loads = [
        pltpu.make_async_copy(source, target, load_sem.at[i])
        for i, (source, target) in enumerate(
            (
                (target_hbm, target_ref),
                (store_hbm, store_ref),
                (source_hbm, source_ref),
                (state_hbm, state_ref),
                (local_hbm, local_ref),
                (links_hbm, links_ref),
                (wet_hbm, wet_ref),
            )
        )
    ]
    for load in loads:
        load.start()

    def place(to_band, to_peer):
        return {"tile": to_band, "sub": to_peer // lanes, "lane": to_peer % lanes}

    def each_other(body):
        def one(offset, carry):
            other = lax.rem(me + offset, total)
            body(other // peers, other % peers)
            return carry

        lax.fori_loop(1, total, one, 0, unroll=total <= 16)

    barrier = pltpu.get_barrier_semaphore()

    def greet(to_band, to_peer):
        pl.semaphore_signal(
            barrier, inc=1, device_id=place(to_band, to_peer), device_id_type=MESH
        )

    each_other(greet)

    def wait_for(ref, length, sem):
        view = ref.at[pl.ds(0, length)]
        pltpu.make_async_copy(view, view, sem).wait()

    wide_id = lax.broadcasted_iota(jnp.int32, (size, size), 1)

    for q in range(3):
        for t in range(slots):
            prim[q, t, pl.ds(size, 8)] = jnp.zeros((8, size), jnp.float32)
    for t in range(slots):
        bed[t, pl.ds(size, 8)] = jnp.zeros((8, size), jnp.float32)
        rim[t] = jnp.zeros((size, size), jnp.float32)
    msgs[...] = jnp.zeros_like(msgs)
    edge_msgs[...] = jnp.zeros_like(edge_msgs)

    loads[0].wait()
    loads[1].wait()
    sides = jnp.zeros((size, size), jnp.float32)
    for r in range(bands):
        block = jnp.int32(0)
        for j in range(bands):
            block = jnp.where(target_ref[j] == r, j, block)
        level = store_ref[0, block]
        out_bed[r] = level
        out_rough[r] = store_ref[1, block]
        level = level.astype(jnp.float32)
        sides = jnp.where(wide_id // 2 == r, pltpu.roll(level, 1 + 2 * r, axis=1), sides)
        if r > 0:
            edge_msgs[r - 1, pl.ds(2, 1)] = level[0:1]
        if r < bands - 1:
            edge_msgs[r + 1, pl.ds(3, 1)] = level[size - 1 : size]
    sides = jnp.transpose(sides)
    loads[2].wait()
    for r in range(bands):
        edge_msgs[r, pl.ds(0, 1)] = sides[2 * r + 1 : 2 * r + 2]
        edge_msgs[r, pl.ds(1, 1)] = sides[2 * r : 2 * r + 1]
    in_bed[band] = out_bed[band]
    in_rough[band] = out_rough[band]
    edge_in[me] = edge_msgs[band]
    for load in loads[3:]:
        load.wait()

    chunks = size // ROWS
    lane_id = lax.broadcasted_iota(jnp.int32, (ROWS, size), 1)

    def edge_columns(t, rows, q, value, before):
        rolled = pltpu.roll(value, 1 + 2 * q, axis=1)
        return jnp.where(lane_id // 2 == q, rolled, before)

    def first(i, carry):
        t = i // chunks
        rows = pl.ds(pl.multiple_of((i % chunks) * ROWS, ROWS), ROWS)
        h = state_ref[0, t, rows]
        inv = 1.0 / h
        u = state_ref[1, t, rows] * inv
        v = state_ref[2, t, rows] * inv
        prim[1, t, rows] = u
        prim[2, t, rows] = v
        value = edge_columns(t, rows, 0, h, jnp.zeros_like(h))
        value = edge_columns(t, rows, 1, u, value)
        value = edge_columns(t, rows, 2, v, value)
        z = local_ref[0, t, rows].astype(jnp.float32)
        columns[t, rows] = edge_columns(t, rows, 3, z, value)
        return carry

    lax.fori_loop(0, slots * chunks, first, 0)

    def send_strips(step):
        current = state_ref if step == 0 else fields
        for t in range(slots):
            turned = jnp.transpose(columns[t])
            for q in range(4):
                if q == 3 and step > 0:
                    continue
                if q == 0:
                    top, low = current[0, t, pl.ds(0, 1)], current[0, t, pl.ds(size - 1, 1)]
                elif q == 3:
                    level = local_ref[0, t].astype(jnp.float32)
                    top, low = level[0:1], level[size - 1 : size]
                else:
                    top, low = prim[q, t, pl.ds(0, 1)], prim[q, t, pl.ds(size - 1, 1)]
                strip = (turned[2 * q + 1 : 2 * q + 2], turned[2 * q : 2 * q + 1], top, low)
                for f in range(4):
                    own[q, pl.ds(f * slots + t, 1)] = strip[f]
                    sent = strip[f]
                    if q == 3:
                        code = CODE * (source_ref[t].astype(jnp.float32) + 1.0)
                        sent = jnp.where(source_ref[t] >= 0, code, sent)
                    msgs[step, f, pl.ds(4 * t + q, 1)] = sent
        strips_x[step][peer] = msgs[step, pl.ds(0, 2)]
        if step == 0:
            pl.semaphore_wait(barrier, total - 1)

        def send(kind, source, target, to_band, to_peer):
            pltpu.make_async_remote_copy(
                src_ref=source,
                dst_ref=target.at[peer],
                send_sem=strip_send.at[step, kind],
                recv_sem=strip_recv.at[step, kind],
                device_id=place(to_band, to_peer),
                device_id_type=MESH,
            ).start()

        @pl.when(has_south)
        def _():
            for offset in range(peers):
                to_peer = lax.rem(peer + offset, peers)
                send(1, msgs.at[step, 3], strips_n[step], band + 1, to_peer)

        @pl.when(has_north)
        def _():
            for offset in range(peers):
                to_peer = lax.rem(peer + offset, peers)
                send(2, msgs.at[step, 2], strips_s[step], band - 1, to_peer)

        for offset in range(1, peers):
            to_peer = lax.rem(peer + offset, peers)
            send(0, msgs.at[step, pl.ds(0, 2)], strips_x[step], band, to_peer)

    def inner(i, carry):
        t = i // chunks
        start = pl.multiple_of((i % chunks) * ROWS, ROWS)
        rows = pl.ds(start, ROWS)
        below = pl.ds(start + 1, ROWS)
        eta, u, v, z = prim[0, t, rows], prim[1, t, rows], prim[2, t, rows], bed[t, rows]
        east = [pltpu.roll(x, size - 1, axis=1) for x in (eta, z, u, v)]
        mass, base, press, tang = face_flux(eta, z, u, v, *east)
        inside = lane_id < size - 1
        mass = jnp.where(inside, mass, 0.0)
        far = jnp.where(inside, base + press, 0.0)
        near = jnp.where(inside, base - press, 0.0)
        tang = jnp.where(inside, tang, 0.0)
        tend[0, t, rows] = mass - pltpu.roll(mass, 1, axis=1)
        tend[1, t, rows] = far - pltpu.roll(near, 1, axis=1)
        tend[2, t, rows] = tang - pltpu.roll(tang, 1, axis=1)
        mass, base, press, tang = face_flux(
            eta, z, v, u, prim[0, t, below], bed[t, below], prim[2, t, below], prim[1, t, below]
        )
        into = pl.ds(pl.multiple_of(start + 8, 8), ROWS)
        faces[0, t, into] = mass
        faces[1, t, into] = base + press
        faces[2, t, into] = base - press
        faces[3, t, into] = tang
        return carry

    def wait_strips(step):
        if peers > 1:
            wait_for(strips_x[step], peers - 1, strip_recv.at[step, 0])

        @pl.when(has_north)
        def _():
            wait_for(strips_n[step], peers, strip_recv.at[step, 1])

        @pl.when(has_south)
        def _():
            wait_for(strips_s[step], peers, strip_recv.at[step, 2])

    def rims(step):
        for t in range(slots):
            for f in range(4):
                device = links_ref[t, 0, f]
                linked = device >= 0
                who = lax.rem(jnp.maximum(device, 0), peers)
                slot = jnp.maximum(links_ref[t, 1, f], 0)
                rows = pl.ds(4 * slot, 4)
                if f < 2:
                    remote = strips_x[step][who, 1 - f, rows]
                else:
                    remote = (strips_n if f == 2 else strips_s)[step][who, rows]
                row = pl.ds(f * slots + t, 1)
                if step == 0:
                    told = remote[3:4]
                    level = told
                    for r in range(bands):
                        edge = edge_in[r * peers + who, pl.ds((1, 0, 3, 2)[f], 1)]
                        level = jnp.where(told == CODE * (r + 1.0), edge, level)
                    ghost[3, row] = jnp.where(linked, level, own[3, row])
                for q in range(3):
                    mine = own[q, row]
                    if q == (1 if f < 2 else 2):
                        mine = -mine
                    ghost[q, row] = jnp.where(linked, remote[q : q + 1], mine)
        row_id = lax.broadcasted_iota(jnp.int32, (4 * slots, size), 0) // slots
        near_side = row_id % 2 == 0
        across = row_id < 2
        g = [ghost[q] for q in range(4)]
        o = [own[q] for q in range(4)]

        def ordered(x):
            h, u, v, z = x
            return h + z, z, jnp.where(across, u, v), jnp.where(across, v, u)

        go, oo = ordered(g), ordered(o)
        left = [jnp.where(near_side, a, b) for a, b in zip(go, oo)]
        right = [jnp.where(near_side, b, a) for a, b in zip(go, oo)]
        mass, base, press, tang = face_flux(*left, *right)
        normal = jnp.where(near_side, base - press, base + press)

        def pick(value, f, t):
            return value[f * slots + t : f * slots + t + 1]

        for t in range(slots):
            for q, value in enumerate((mass, normal, tang)):
                rim[t, pl.ds(2 * q, 1)] = pick(value, 1, t)
                rim[t, pl.ds(2 * q + 1, 1)] = -pick(value, 0, t)
            top, low = pl.ds(7, 1), pl.ds(7 + size, 1)
            faces[0, t, top] = pick(mass, 2, t)
            faces[2, t, top] = pick(normal, 2, t)
            faces[3, t, top] = pick(tang, 2, t)
            faces[0, t, low] = pick(mass, 3, t)
            faces[1, t, low] = pick(normal, 3, t)
            faces[3, t, low] = pick(tang, 3, t)
            rim_t[t] = jnp.transpose(rim[t])

    def update(step, i, carry):
        last = step == STEPS - 1
        current = state_ref if step == 0 else fields
        t = i // chunks
        start = pl.multiple_of((i % chunks) * ROWS, ROWS)
        rows = pl.ds(start, ROWS)
        here = pl.ds(pl.multiple_of(start + 8, 8), ROWS)
        above = pl.ds(start + 7, ROWS)
        turned = rim_t[t, rows]
        border = (lane_id == 0) | (lane_id == size - 1)

        def sides(q):
            return jnp.where(border, pltpu.roll(turned, size - 1 - 2 * q, axis=1), 0.0)

        ratio = 0.5 * DT / CELL
        h = current[0, t, rows] - ratio * (
            tend[0, t, rows] + sides(0) + (faces[0, t, here] - faces[0, t, above])
        )
        qx = current[1, t, rows] - ratio * (
            tend[1, t, rows] + sides(1) + (faces[3, t, here] - faces[3, t, above])
        )
        qy = current[2, t, rows] - ratio * (
            tend[2, t, rows] + sides(2) + (faces[1, t, here] - faces[2, t, above])
        )
        power = jnp.exp((-7.0 / 3.0) * jnp.log(h))
        damp = 1.0 / (1.0 + drag[t, rows] * root(qx * qx + qy * qy) * power)
        qx = qx * damp
        qy = qy * damp
        if last:
            live = t < wet_ref[0]
            out_ref[0, t, rows] = jnp.where(live, h, 0.0)
            out_ref[1, t, rows] = jnp.where(live, qx, 0.0)
            out_ref[2, t, rows] = jnp.where(live, qy, 0.0)
        else:
            fields[0, t, rows] = h
            fields[1, t, rows] = qx
            fields[2, t, rows] = qy
            inv = 1.0 / h
            u = qx * inv
            v = qy * inv
            prim[0, t, rows] = h + bed[t, rows]
            prim[1, t, rows] = u
            prim[2, t, rows] = v
            value = edge_columns(t, rows, 0, h, jnp.zeros_like(h))
            value = edge_columns(t, rows, 1, u, value)
            columns[t, rows] = edge_columns(t, rows, 2, v, value)
        return carry

    def send_terrain():
        def send_edges(to_band, to_peer):
            pltpu.make_async_remote_copy(
                src_ref=edge_msgs.at[to_band],
                dst_ref=edge_in.at[me],
                send_sem=terrain_send.at[2],
                recv_sem=terrain_recv.at[2],
                device_id=place(to_band, to_peer),
                device_id_type=MESH,
            ).start()

        each_other(send_edges)
        for part, (source, target) in enumerate(((out_bed, in_bed), (out_rough, in_rough))):
            for offset in range(1, bands):
                to_band = lax.rem(band + offset, bands)
                pltpu.make_async_remote_copy(
                    src_ref=source.at[to_band],
                    dst_ref=target.at[band],
                    send_sem=terrain_send.at[part],
                    recv_sem=terrain_recv.at[part],
                    device_id=place(to_band, peer),
                    device_id_type=MESH,
                ).start()

    def fill_bed():
        wait_for(in_bed, bands - 1, terrain_recv.at[0])
        for t in range(slots):
            fetched = in_bed[jnp.maximum(source_ref[t], 0)].astype(jnp.float32)
            level = jnp.where(source_ref[t] >= 0, fetched, local_ref[0, t].astype(jnp.float32))
            bed[t, pl.ds(0, size)] = level
            prim[0, t, pl.ds(0, size)] = level + state_ref[0, t]
            own[3, pl.ds(2 * slots + t, 1)] = level[0:1]
            own[3, pl.ds(3 * slots + t, 1)] = level[size - 1 : size]

    def own_edges():
        wait_for(edge_in, total - 1, terrain_recv.at[2])
        for t in range(slots):
            holder = jnp.maximum(source_ref[t], 0) * peers + peer
            for f in range(2):
                row = pl.ds(f * slots + t, 1)
                edge = edge_in[holder, pl.ds(f, 1)]
                own[3, row] = jnp.where(source_ref[t] >= 0, edge, own[3, row])

    def fill_drag():
        wait_for(in_rough, bands - 1, terrain_recv.at[1])
        for t in range(slots):
            fetched = in_rough[jnp.maximum(source_ref[t], 0)].astype(jnp.float32)
            rough = jnp.where(source_ref[t] >= 0, fetched, local_ref[1, t].astype(jnp.float32))
            drag[t] = (DT * GRAVITY) * rough * rough

    for step in range(STEPS):
        send_strips(step)
        if step == 0:
            send_terrain()
            fill_bed()
        lax.fori_loop(0, slots * chunks, inner, 0)
        wait_strips(step)
        if step == 0:
            own_edges()
        rims(step)
        if step == 0:
            fill_drag()
        lax.fori_loop(0, slots * chunks, functools.partial(update, step), 0)

    wait_for(edge_in, total - 1, terrain_send.at[2])
    wait_for(out_rough, bands - 1, terrain_send.at[1])
    wait_for(out_bed, bands - 1, terrain_send.at[0])
    for step in range(STEPS):
        wait_for(strips_x[step], peers - 1, strip_send.at[step, 0])

        @pl.when(has_south)
        def _():
            wait_for(strips_n[step], peers, strip_send.at[step, 1])

        @pl.when(has_north)
        def _():
            wait_for(strips_s[step], peers, strip_send.at[step, 2])


def local(sizes, state, terrain_local, terrain_store, wet_count, face_links, new_source, store_target):
    bands, subs, lanes, slots, size = sizes
    peers = subs * lanes
    f32, bf16 = jnp.float32, jnp.bfloat16
    block = (bands, size, size)
    hbm = pl.BlockSpec(memory_space=pltpu.HBM)
    vmem = pl.BlockSpec(memory_space=pltpu.VMEM)
    msg = (4 * slots, size)
    return pl.pallas_call(
        functools.partial(kernel, sizes),
        out_shape=jax.ShapeDtypeStruct(state.shape, f32),
        in_specs=[hbm] * 7,
        out_specs=vmem,
        scratch_shapes=[
            pltpu.SMEM(wet_count.shape, jnp.int32),
            pltpu.SMEM(face_links.shape, jnp.int32),
            pltpu.SMEM(new_source.shape, jnp.int32),
            pltpu.SMEM(store_target.shape, jnp.int32),
            pltpu.VMEM(state.shape, f32),
            pltpu.VMEM(terrain_local.shape, bf16),
            pltpu.VMEM(terrain_store.shape, bf16),
            pltpu.VMEM(block, bf16),
            pltpu.VMEM(block, bf16),
            pltpu.VMEM(block, bf16),
            pltpu.VMEM(block, bf16),
            pltpu.VMEM((slots, size + 8, size), f32),
            pltpu.VMEM((slots, size, size), f32),
            pltpu.VMEM((3, slots, size, size), f32),
            pltpu.VMEM((3, slots, size + 8, size), f32),
            pltpu.VMEM((4, slots, size + 16, size), f32),
            pltpu.VMEM((3, slots, size, size), f32),
            pltpu.VMEM((slots, size, size), f32),
            pltpu.VMEM((slots, size, size), f32),
            pltpu.VMEM((slots, size, size), f32),
            pltpu.VMEM((4,) + msg, f32),
            pltpu.VMEM((4,) + msg, f32),
            pltpu.VMEM((STEPS, 4) + msg, f32),
            [pltpu.VMEM((peers, 2) + msg, f32) for _ in range(STEPS)],
            [pltpu.VMEM((peers,) + msg, f32) for _ in range(STEPS)],
            [pltpu.VMEM((peers,) + msg, f32) for _ in range(STEPS)],
            pltpu.VMEM((bands, 4, size), f32),
            pltpu.VMEM((bands * peers, 4, size), f32),
            pltpu.SemaphoreType.DMA((7,)),
            pltpu.SemaphoreType.DMA((3,)),
            pltpu.SemaphoreType.DMA((3,)),
            pltpu.SemaphoreType.DMA((STEPS, 3)),
            pltpu.SemaphoreType.DMA((STEPS, 3)),
        ],
        compiler_params=pltpu.CompilerParams(
            collective_id=0, has_side_effects=True, vmem_limit_bytes=64 * 1024 * 1024
        ),
    )(wet_count, face_links, new_source, store_target, state, terrain_local, terrain_store)


def solution(mesh):
    shape = mesh.shape
    devices = P(None, AXES, None, None)
    flat = P(AXES)

    def whole(state, *rest):
        def part(block, *others):
            sizes = (shape["tile"], shape["sub"], shape["lane"], block.shape[1], block.shape[2])
            return local(sizes, block, *others)

        return jax.shard_map(
            part,
            mesh=mesh,
            in_specs=(devices, devices, devices, flat, P(AXES, None, None), flat, flat),
            out_specs=devices,
            check_vma=False,
        )(state, *rest)

    return whole
```

```python
import functools

import jax
import jax.numpy as jnp
from jax import lax
from jax.experimental import pallas as pl
from jax.experimental.pallas import tpu as pltpu
from jax.sharding import PartitionSpec as P

STEPS = 3
GRAVITY = 9.81
CELL = 30.0
DT = 1.0
ROWS = 128
CODE = 4096.0
AXES = ("region", "tile", "sub", "lane")
MESH = pl.DeviceIdType.MESH


def root(x):
    return x * lax.rsqrt(jnp.maximum(x, 1.2e-38))


def face_flux(eta_l, z_l, n_l, t_l, eta_r, z_r, n_r, t_r):
    z_face = jnp.maximum(z_l, z_r)
    h_l = jnp.maximum(eta_l - z_face, 0.0)
    h_r = jnp.maximum(eta_r - z_face, 0.0)
    wave = jnp.maximum(
        jnp.abs(n_l) + root(GRAVITY * h_l), jnp.abs(n_r) + root(GRAVITY * h_r)
    )
    m_l = h_l * n_l
    m_r = h_r * n_r
    d = h_r - h_l
    mass = (m_l + m_r) - wave * d
    base = (m_l * n_l + m_r * n_r) - wave * (m_r - m_l)
    press = (0.5 * GRAVITY) * d * (h_r + h_l)
    tang = (m_l * t_l + m_r * t_r) - wave * (h_r * t_r - h_l * t_l)
    return mass, base, press, tang


def kernel(
    sizes,
    wet_hbm,
    links_hbm,
    source_hbm,
    target_hbm,
    state_hbm,
    local_hbm,
    store_hbm,
    out_ref,
    wet_ref,
    links_ref,
    source_ref,
    target_ref,
    state_ref,
    local_ref,
    store_ref,
    out_bed,
    out_rough,
    in_bed,
    in_rough,
    bed,
    drag,
    fields,
    prim,
    faces,
    tend,
    columns,
    rim,
    rim_t,
    own,
    ghost,
    msgs,
    strips_x,
    strips_n,
    strips_s,
    edge_msgs,
    edge_in,
    load_sem,
    terrain_send,
    terrain_recv,
    strip_send,
    strip_recv,
):
    bands, subs, lanes, slots, size = sizes
    peers = subs * lanes
    total = bands * peers
    band = lax.axis_index("tile")
    peer = lax.axis_index("sub") * lanes + lax.axis_index("lane")
    me = band * peers + peer
    has_north = band > 0
    has_south = band < bands - 1

    loads = [
        pltpu.make_async_copy(source, target, load_sem.at[i])
        for i, (source, target) in enumerate(
            (
                (target_hbm, target_ref),
                (store_hbm, store_ref),
                (source_hbm, source_ref),
                (state_hbm, state_ref),
                (local_hbm, local_ref),
                (links_hbm, links_ref),
                (wet_hbm, wet_ref),
            )
        )
    ]
    for load in loads:
        load.start()

    def place(to_band, to_peer):
        return {"tile": to_band, "sub": to_peer // lanes, "lane": to_peer % lanes}

    def each_other(body):
        def one(offset, carry):
            other = lax.rem(me + offset, total)
            body(other // peers, other % peers)
            return carry

        lax.fori_loop(1, total, one, 0, unroll=total <= 16)

    barrier = pltpu.get_barrier_semaphore()

    def greet(to_band, to_peer):
        pl.semaphore_signal(
            barrier, inc=1, device_id=place(to_band, to_peer), device_id_type=MESH
        )

    each_other(greet)

    def wait_for(ref, length, sem):
        view = ref.at[pl.ds(0, length)]
        pltpu.make_async_copy(view, view, sem).wait()

    wide_id = lax.broadcasted_iota(jnp.int32, (size, size), 1)

    for q in range(3):
        for t in range(slots):
            prim[q, t, pl.ds(size, 8)] = jnp.zeros((8, size), jnp.float32)
    for t in range(slots):
        bed[t, pl.ds(size, 8)] = jnp.zeros((8, size), jnp.float32)
        rim[t] = jnp.zeros((size, size), jnp.float32)
    msgs[...] = jnp.zeros_like(msgs)
    edge_msgs[...] = jnp.zeros_like(edge_msgs)

    loads[0].wait()
    loads[1].wait()
    sides = jnp.zeros((size, size), jnp.float32)
    for r in range(bands):
        block = jnp.int32(0)
        for j in range(bands):
            block = jnp.where(target_ref[j] == r, j, block)
        level = store_ref[0, block]
        out_bed[r] = level
        out_rough[r] = store_ref[1, block]
        level = level.astype(jnp.float32)
        sides = jnp.where(wide_id // 2 == r, pltpu.roll(level, 1 + 2 * r, axis=1), sides)
        if r > 0:
            edge_msgs[r - 1, pl.ds(2, 1)] = level[0:1]
        if r < bands - 1:
            edge_msgs[r + 1, pl.ds(3, 1)] = level[size - 1 : size]
    sides = jnp.transpose(sides)
    loads[2].wait()
    for r in range(bands):
        edge_msgs[r, pl.ds(0, 1)] = sides[2 * r + 1 : 2 * r + 2]
        edge_msgs[r, pl.ds(1, 1)] = sides[2 * r : 2 * r + 1]
    in_bed[band] = out_bed[band]
    in_rough[band] = out_rough[band]
    edge_in[me] = edge_msgs[band]
    for load in loads[3:]:
        load.wait()

    chunks = size // ROWS
    lane_id = lax.broadcasted_iota(jnp.int32, (ROWS, size), 1)

    def edge_columns(t, rows, q, value, before):
        rolled = pltpu.roll(value, 1 + 2 * q, axis=1)
        return jnp.where(lane_id // 2 == q, rolled, before)

    def first(i, carry):
        t = i // chunks
        rows = pl.ds(pl.multiple_of((i % chunks) * ROWS, ROWS), ROWS)
        h = state_ref[0, t, rows]
        inv = 1.0 / h
        u = state_ref[1, t, rows] * inv
        v = state_ref[2, t, rows] * inv
        prim[1, t, rows] = u
        prim[2, t, rows] = v
        value = edge_columns(t, rows, 0, h, jnp.zeros_like(h))
        value = edge_columns(t, rows, 1, u, value)
        value = edge_columns(t, rows, 2, v, value)
        z = local_ref[0, t, rows].astype(jnp.float32)
        columns[t, rows] = edge_columns(t, rows, 3, z, value)
        return carry

    lax.fori_loop(0, slots * chunks, first, 0)

    def send_strips(step):
        current = state_ref if step == 0 else fields
        for t in range(slots):
            turned = jnp.transpose(columns[t])
            for q in range(4):
                if q == 3 and step > 0:
                    continue
                if q == 0:
                    top, low = current[0, t, pl.ds(0, 1)], current[0, t, pl.ds(size - 1, 1)]
                elif q == 3:
                    level = local_ref[0, t].astype(jnp.float32)
                    top, low = level[0:1], level[size - 1 : size]
                else:
                    top, low = prim[q, t, pl.ds(0, 1)], prim[q, t, pl.ds(size - 1, 1)]
                strip = (turned[2 * q + 1 : 2 * q + 2], turned[2 * q : 2 * q + 1], top, low)
                for f in range(4):
                    own[q, pl.ds(f * slots + t, 1)] = strip[f]
                    sent = strip[f]
                    if q == 3:
                        code = CODE * (source_ref[t].astype(jnp.float32) + 1.0)
                        sent = jnp.where(source_ref[t] >= 0, code, sent)
                    msgs[step, f, pl.ds(4 * t + q, 1)] = sent
        strips_x[step][peer] = msgs[step, pl.ds(0, 2)]
        if step == 0:
            pl.semaphore_wait(barrier, total - 1)

        def send(kind, source, target, to_band, to_peer):
            pltpu.make_async_remote_copy(
                src_ref=source,
                dst_ref=target.at[peer],
                send_sem=strip_send.at[step, kind],
                recv_sem=strip_recv.at[step, kind],
                device_id=place(to_band, to_peer),
                device_id_type=MESH,
            ).start()

        @pl.when(has_south)
        def _():
            for offset in range(peers):
                to_peer = lax.rem(peer + offset, peers)
                send(1, msgs.at[step, 3], strips_n[step], band + 1, to_peer)

        @pl.when(has_north)
        def _():
            for offset in range(peers):
                to_peer = lax.rem(peer + offset, peers)
                send(2, msgs.at[step, 2], strips_s[step], band - 1, to_peer)

        for offset in range(1, peers):
            to_peer = lax.rem(peer + offset, peers)
            send(0, msgs.at[step, pl.ds(0, 2)], strips_x[step], band, to_peer)

    def inner(i, carry):
        t = i // chunks
        start = pl.multiple_of((i % chunks) * ROWS, ROWS)
        rows = pl.ds(start, ROWS)
        below = pl.ds(start + 1, ROWS)
        eta, u, v, z = prim[0, t, rows], prim[1, t, rows], prim[2, t, rows], bed[t, rows]
        east = [pltpu.roll(x, size - 1, axis=1) for x in (eta, z, u, v)]
        mass, base, press, tang = face_flux(eta, z, u, v, *east)
        inside = lane_id < size - 1
        mass = jnp.where(inside, mass, 0.0)
        far = jnp.where(inside, base + press, 0.0)
        near = jnp.where(inside, base - press, 0.0)
        tang = jnp.where(inside, tang, 0.0)
        tend[0, t, rows] = mass - pltpu.roll(mass, 1, axis=1)
        tend[1, t, rows] = far - pltpu.roll(near, 1, axis=1)
        tend[2, t, rows] = tang - pltpu.roll(tang, 1, axis=1)
        mass, base, press, tang = face_flux(
            eta, z, v, u, prim[0, t, below], bed[t, below], prim[2, t, below], prim[1, t, below]
        )
        into = pl.ds(pl.multiple_of(start + 8, 8), ROWS)
        faces[0, t, into] = mass
        faces[1, t, into] = base + press
        faces[2, t, into] = base - press
        faces[3, t, into] = tang
        return carry

    def wait_strips(step):
        if peers > 1:
            wait_for(strips_x[step], peers - 1, strip_recv.at[step, 0])

        @pl.when(has_north)
        def _():
            wait_for(strips_n[step], peers, strip_recv.at[step, 1])

        @pl.when(has_south)
        def _():
            wait_for(strips_s[step], peers, strip_recv.at[step, 2])

    def rims(step):
        for t in range(slots):
            for f in range(4):
                device = links_ref[t, 0, f]
                linked = device >= 0
                who = lax.rem(jnp.maximum(device, 0), peers)
                slot = jnp.maximum(links_ref[t, 1, f], 0)
                rows = pl.ds(4 * slot, 4)
                if f < 2:
                    remote = strips_x[step][who, 1 - f, rows]
                else:
                    remote = (strips_n if f == 2 else strips_s)[step][who, rows]
                row = pl.ds(f * slots + t, 1)
                if step == 0:
                    told = remote[3:4]
                    level = told
                    for r in range(bands):
                        edge = edge_in[r * peers + who, pl.ds((1, 0, 3, 2)[f], 1)]
                        level = jnp.where(told == CODE * (r + 1.0), edge, level)
                    ghost[3, row] = jnp.where(linked, level, own[3, row])
                for q in range(3):
                    mine = own[q, row]
                    if q == (1 if f < 2 else 2):
                        mine = -mine
                    ghost[q, row] = jnp.where(linked, remote[q : q + 1], mine)
        row_id = lax.broadcasted_iota(jnp.int32, (4 * slots, size), 0) // slots
        near_side = row_id % 2 == 0
        across = row_id < 2
        g = [ghost[q] for q in range(4)]
        o = [own[q] for q in range(4)]

        def ordered(x):
            h, u, v, z = x
            return h + z, z, jnp.where(across, u, v), jnp.where(across, v, u)

        go, oo = ordered(g), ordered(o)
        left = [jnp.where(near_side, a, b) for a, b in zip(go, oo)]
        right = [jnp.where(near_side, b, a) for a, b in zip(go, oo)]
        mass, base, press, tang = face_flux(*left, *right)
        normal = jnp.where(near_side, base - press, base + press)

        def pick(value, f, t):
            return value[f * slots + t : f * slots + t + 1]

        for t in range(slots):
            for q, value in enumerate((mass, normal, tang)):
                rim[t, pl.ds(2 * q, 1)] = pick(value, 1, t)
                rim[t, pl.ds(2 * q + 1, 1)] = -pick(value, 0, t)
            top, low = pl.ds(7, 1), pl.ds(7 + size, 1)
            faces[0, t, top] = pick(mass, 2, t)
            faces[2, t, top] = pick(normal, 2, t)
            faces[3, t, top] = pick(tang, 2, t)
            faces[0, t, low] = pick(mass, 3, t)
            faces[1, t, low] = pick(normal, 3, t)
            faces[3, t, low] = pick(tang, 3, t)
            rim_t[t] = jnp.transpose(rim[t])

    def update(step, i, carry):
        last = step == STEPS - 1
        current = state_ref if step == 0 else fields
        t = i // chunks
        start = pl.multiple_of((i % chunks) * ROWS, ROWS)
        rows = pl.ds(start, ROWS)
        here = pl.ds(pl.multiple_of(start + 8, 8), ROWS)
        above = pl.ds(start + 7, ROWS)
        turned = rim_t[t, rows]
        border = (lane_id == 0) | (lane_id == size - 1)

        def sides(q):
            return jnp.where(border, pltpu.roll(turned, size - 1 - 2 * q, axis=1), 0.0)

        ratio = 0.5 * DT / CELL
        h = current[0, t, rows] - ratio * (
            tend[0, t, rows] + sides(0) + (faces[0, t, here] - faces[0, t, above])
        )
        qx = current[1, t, rows] - ratio * (
            tend[1, t, rows] + sides(1) + (faces[3, t, here] - faces[3, t, above])
        )
        qy = current[2, t, rows] - ratio * (
            tend[2, t, rows] + sides(2) + (faces[1, t, here] - faces[2, t, above])
        )
        power = jnp.exp((-7.0 / 3.0) * jnp.log(h))
        damp = 1.0 / (1.0 + drag[t, rows] * root(qx * qx + qy * qy) * power)
        qx = qx * damp
        qy = qy * damp
        if last:
            live = t < wet_ref[0]
            out_ref[0, t, rows] = jnp.where(live, h, 0.0)
            out_ref[1, t, rows] = jnp.where(live, qx, 0.0)
            out_ref[2, t, rows] = jnp.where(live, qy, 0.0)
        else:
            fields[0, t, rows] = h
            fields[1, t, rows] = qx
            fields[2, t, rows] = qy
            inv = 1.0 / h
            u = qx * inv
            v = qy * inv
            prim[0, t, rows] = h + bed[t, rows]
            prim[1, t, rows] = u
            prim[2, t, rows] = v
            value = edge_columns(t, rows, 0, h, jnp.zeros_like(h))
            value = edge_columns(t, rows, 1, u, value)
            columns[t, rows] = edge_columns(t, rows, 2, v, value)
        return carry

    def send_terrain():
        def send_edges(to_band, to_peer):
            pltpu.make_async_remote_copy(
                src_ref=edge_msgs.at[to_band],
                dst_ref=edge_in.at[me],
                send_sem=terrain_send.at[2],
                recv_sem=terrain_recv.at[2],
                device_id=place(to_band, to_peer),
                device_id_type=MESH,
            ).start()

        each_other(send_edges)
        for part, (source, target) in enumerate(((out_bed, in_bed), (out_rough, in_rough))):
            for offset in range(1, bands):
                to_band = lax.rem(band + offset, bands)
                pltpu.make_async_remote_copy(
                    src_ref=source.at[to_band],
                    dst_ref=target.at[band],
                    send_sem=terrain_send.at[part],
                    recv_sem=terrain_recv.at[part],
                    device_id=place(to_band, peer),
                    device_id_type=MESH,
                ).start()

    def fill_bed():
        wait_for(in_bed, bands - 1, terrain_recv.at[0])
        for t in range(slots):
            fetched = in_bed[jnp.maximum(source_ref[t], 0)].astype(jnp.float32)
            level = jnp.where(source_ref[t] >= 0, fetched, local_ref[0, t].astype(jnp.float32))
            bed[t, pl.ds(0, size)] = level
            prim[0, t, pl.ds(0, size)] = level + state_ref[0, t]
            own[3, pl.ds(2 * slots + t, 1)] = level[0:1]
            own[3, pl.ds(3 * slots + t, 1)] = level[size - 1 : size]

    def own_edges():
        wait_for(edge_in, total - 1, terrain_recv.at[2])
        for t in range(slots):
            holder = jnp.maximum(source_ref[t], 0) * peers + peer
            for f in range(2):
                row = pl.ds(f * slots + t, 1)
                edge = edge_in[holder, pl.ds(f, 1)]
                own[3, row] = jnp.where(source_ref[t] >= 0, edge, own[3, row])

    def fill_drag():
        wait_for(in_rough, bands - 1, terrain_recv.at[1])
        for t in range(slots):
            fetched = in_rough[jnp.maximum(source_ref[t], 0)].astype(jnp.float32)
            rough = jnp.where(source_ref[t] >= 0, fetched, local_ref[1, t].astype(jnp.float32))
            drag[t] = (DT * GRAVITY) * rough * rough

    for step in range(STEPS):
        send_strips(step)
        if step == 0:
            send_terrain()
            fill_bed()
        lax.fori_loop(0, slots * chunks, inner, 0)
        wait_strips(step)
        if step == 0:
            own_edges()
        rims(step)
        if step == 0:
            fill_drag()
        lax.fori_loop(0, slots * chunks, functools.partial(update, step), 0)

    wait_for(edge_in, total - 1, terrain_send.at[2])
    wait_for(out_rough, bands - 1, terrain_send.at[1])
    wait_for(out_bed, bands - 1, terrain_send.at[0])
    for step in range(STEPS):
        wait_for(strips_x[step], peers - 1, strip_send.at[step, 0])

        @pl.when(has_south)
        def _():
            wait_for(strips_n[step], peers, strip_send.at[step, 1])

        @pl.when(has_north)
        def _():
            wait_for(strips_s[step], peers, strip_send.at[step, 2])


def local(sizes, state, terrain_local, terrain_store, wet_count, face_links, new_source, store_target):
    bands, subs, lanes, slots, size = sizes
    peers = subs * lanes
    f32, bf16 = jnp.float32, jnp.bfloat16
    block = (bands, size, size)
    hbm = pl.BlockSpec(memory_space=pltpu.HBM)
    vmem = pl.BlockSpec(memory_space=pltpu.VMEM)
    msg = (4 * slots, size)
    return pl.pallas_call(
        functools.partial(kernel, sizes),
        out_shape=pltpu.VMEM(state.shape, f32),
        in_specs=[hbm] * 7,
        out_specs=vmem,
        scratch_shapes=[
            pltpu.SMEM(wet_count.shape, jnp.int32),
            pltpu.SMEM(face_links.shape, jnp.int32),
            pltpu.SMEM(new_source.shape, jnp.int32),
            pltpu.SMEM(store_target.shape, jnp.int32),
            pltpu.VMEM(state.shape, f32),
            pltpu.VMEM(terrain_local.shape, bf16),
            pltpu.VMEM(terrain_store.shape, bf16),
            pltpu.VMEM(block, bf16),
            pltpu.VMEM(block, bf16),
            pltpu.VMEM(block, bf16),
            pltpu.VMEM(block, bf16),
            pltpu.VMEM((slots, size + 8, size), f32),
            pltpu.VMEM((slots, size, size), f32),
            pltpu.VMEM((3, slots, size, size), f32),
            pltpu.VMEM((3, slots, size + 8, size), f32),
            pltpu.VMEM((4, slots, size + 16, size), f32),
            pltpu.VMEM((3, slots, size, size), f32),
            pltpu.VMEM((slots, size, size), f32),
            pltpu.VMEM((slots, size, size), f32),
            pltpu.VMEM((slots, size, size), f32),
            pltpu.VMEM((4,) + msg, f32),
            pltpu.VMEM((4,) + msg, f32),
            pltpu.VMEM((STEPS, 4) + msg, f32),
            [pltpu.VMEM((peers, 2) + msg, f32) for _ in range(STEPS)],
            [pltpu.VMEM((peers,) + msg, f32) for _ in range(STEPS)],
            [pltpu.VMEM((peers,) + msg, f32) for _ in range(STEPS)],
            pltpu.VMEM((bands, 4, size), f32),
            pltpu.VMEM((bands * peers, 4, size), f32),
            pltpu.SemaphoreType.DMA((7,)),
            pltpu.SemaphoreType.DMA((3,)),
            pltpu.SemaphoreType.DMA((3,)),
            pltpu.SemaphoreType.DMA((STEPS, 3)),
            pltpu.SemaphoreType.DMA((STEPS, 3)),
        ],
        compiler_params=pltpu.CompilerParams(
            collective_id=0, has_side_effects=True, vmem_limit_bytes=63 * 1024 * 1024
        ),
    )(wet_count, face_links, new_source, store_target, state, terrain_local, terrain_store)


def solution(mesh):
    shape = mesh.shape
    devices = P(None, AXES, None, None)
    flat = P(AXES)

    def whole(state, *rest):
        def part(block, *others):
            sizes = (shape["tile"], shape["sub"], shape["lane"], block.shape[1], block.shape[2])
            return local(sizes, block, *others)

        return jax.shard_map(
            part,
            mesh=mesh,
            in_specs=(devices, devices, devices, flat, P(AXES, None, None), flat, flat),
            out_specs=devices,
            check_vma=False,
        )(state, *rest)

    return whole
```

```python
import functools

import jax
import jax.numpy as jnp
from jax import lax
from jax.experimental import pallas as pl
from jax.experimental.pallas import tpu as pltpu
from jax.sharding import PartitionSpec as P

STEPS = 3
GRAVITY = 9.81
CELL = 30.0
DT = 1.0
ROWS = 128
CODE = 4096.0
AXES = ("region", "tile", "sub", "lane")
MESH = pl.DeviceIdType.MESH


def root(x):
    return x * lax.rsqrt(jnp.maximum(x, 1.2e-38))


def face_flux(eta_l, z_l, n_l, t_l, eta_r, z_r, n_r, t_r):
    z_face = jnp.maximum(z_l, z_r)
    h_l = jnp.maximum(eta_l - z_face, 0.0)
    h_r = jnp.maximum(eta_r - z_face, 0.0)
    wave = jnp.maximum(
        jnp.abs(n_l) + root(GRAVITY * h_l), jnp.abs(n_r) + root(GRAVITY * h_r)
    )
    m_l = h_l * n_l
    m_r = h_r * n_r
    d = h_r - h_l
    mass = (m_l + m_r) - wave * d
    base = (m_l * n_l + m_r * n_r) - wave * (m_r - m_l)
    press = (0.5 * GRAVITY) * d * (h_r + h_l)
    tang = (m_l * t_l + m_r * t_r) - wave * (h_r * t_r - h_l * t_l)
    return mass, base, press, tang


def kernel(
    sizes,
    wet_hbm,
    links_hbm,
    source_hbm,
    target_hbm,
    state_hbm,
    local_hbm,
    store_hbm,
    out_ref,
    wet_ref,
    links_ref,
    source_ref,
    target_ref,
    state_ref,
    local_ref,
    store_ref,
    out_bed,
    out_rough,
    in_bed,
    in_rough,
    bed,
    drag,
    fields,
    prim,
    faces,
    tend,
    columns,
    rim,
    rim_t,
    own,
    ghost,
    msgs,
    strips_x,
    strips_n,
    strips_s,
    edge_msgs,
    edge_in,
    load_sem,
    terrain_send,
    terrain_recv,
    strip_send,
    strip_recv,
):
    bands, subs, lanes, slots, size = sizes
    peers = subs * lanes
    total = bands * peers
    band = lax.axis_index("tile")
    peer = lax.axis_index("sub") * lanes + lax.axis_index("lane")
    me = band * peers + peer
    has_north = band > 0
    has_south = band < bands - 1

    loads = [
        pltpu.make_async_copy(source, target, load_sem.at[i])
        for i, (source, target) in enumerate(
            (
                (target_hbm, target_ref),
                (store_hbm, store_ref),
                (source_hbm, source_ref),
                (state_hbm, state_ref),
                (local_hbm, local_ref),
                (links_hbm, links_ref),
                (wet_hbm, wet_ref),
            )
        )
    ]
    for load in loads:
        load.start()

    def place(to_band, to_peer):
        return {"tile": to_band, "sub": to_peer // lanes, "lane": to_peer % lanes}

    def each_other(body):
        def one(offset, carry):
            other = lax.rem(me + offset, total)
            body(other // peers, other % peers)
            return carry

        lax.fori_loop(1, total, one, 0, unroll=total <= 16)

    barrier = pltpu.get_barrier_semaphore()

    def greet(to_band, to_peer):
        pl.semaphore_signal(
            barrier, inc=1, device_id=place(to_band, to_peer), device_id_type=MESH
        )

    each_other(greet)

    def wait_for(ref, length, sem):
        view = ref.at[pl.ds(0, length)]
        pltpu.make_async_copy(view, view, sem).wait()

    wide_id = lax.broadcasted_iota(jnp.int32, (size, size), 1)

    for q in range(3):
        for t in range(slots):
            prim[q, t, pl.ds(size, 8)] = jnp.zeros((8, size), jnp.float32)
    for t in range(slots):
        bed[t, pl.ds(size, 8)] = jnp.zeros((8, size), jnp.float32)
        rim[t] = jnp.zeros((size, size), jnp.float32)
    msgs[...] = jnp.zeros_like(msgs)
    edge_msgs[...] = jnp.zeros_like(edge_msgs)

    loads[0].wait()
    loads[1].wait()
    sides = jnp.zeros((size, size), jnp.float32)
    for r in range(bands):
        block = jnp.int32(0)
        for j in range(bands):
            block = jnp.where(target_ref[j] == r, j, block)
        level = store_ref[0, block]
        out_bed[r] = level
        out_rough[r] = store_ref[1, block]
        level = level.astype(jnp.float32)
        sides = jnp.where(wide_id // 2 == r, pltpu.roll(level, 1 + 2 * r, axis=1), sides)
        if r > 0:
            edge_msgs[r - 1, pl.ds(2, 1)] = level[0:1]
        if r < bands - 1:
            edge_msgs[r + 1, pl.ds(3, 1)] = level[size - 1 : size]
    sides = jnp.transpose(sides)
    loads[2].wait()
    for r in range(bands):
        edge_msgs[r, pl.ds(0, 1)] = sides[2 * r + 1 : 2 * r + 2]
        edge_msgs[r, pl.ds(1, 1)] = sides[2 * r : 2 * r + 1]
    in_bed[band] = out_bed[band]
    in_rough[band] = out_rough[band]
    edge_in[me] = edge_msgs[band]
    for load in loads[3:]:
        load.wait()

    chunks = size // ROWS
    lane_id = lax.broadcasted_iota(jnp.int32, (ROWS, size), 1)

    def edge_columns(t, rows, q, value, before):
        rolled = pltpu.roll(value, 1 + 2 * q, axis=1)
        return jnp.where(lane_id // 2 == q, rolled, before)

    def first(i, carry):
        t = i // chunks
        rows = pl.ds(pl.multiple_of((i % chunks) * ROWS, ROWS), ROWS)
        h = state_ref[0, t, rows]
        inv = 1.0 / h
        u = state_ref[1, t, rows] * inv
        v = state_ref[2, t, rows] * inv
        prim[1, t, rows] = u
        prim[2, t, rows] = v
        value = edge_columns(t, rows, 0, h, jnp.zeros_like(h))
        value = edge_columns(t, rows, 1, u, value)
        value = edge_columns(t, rows, 2, v, value)
        z = local_ref[0, t, rows].astype(jnp.float32)
        columns[t, rows] = edge_columns(t, rows, 3, z, value)
        return carry

    lax.fori_loop(0, slots * chunks, first, 0)

    def send_strips(step):
        current = state_ref if step == 0 else fields
        for t in range(slots):
            turned = jnp.transpose(columns[t])
            for q in range(4):
                if q == 3 and step > 0:
                    continue
                if q == 0:
                    top, low = current[0, t, pl.ds(0, 1)], current[0, t, pl.ds(size - 1, 1)]
                elif q == 3:
                    level = local_ref[0, t].astype(jnp.float32)
                    top, low = level[0:1], level[size - 1 : size]
                else:
                    top, low = prim[q, t, pl.ds(0, 1)], prim[q, t, pl.ds(size - 1, 1)]
                strip = (turned[2 * q + 1 : 2 * q + 2], turned[2 * q : 2 * q + 1], top, low)
                for f in range(4):
                    own[q, pl.ds(f * slots + t, 1)] = strip[f]
                    sent = strip[f]
                    if q == 3:
                        code = CODE * (source_ref[t].astype(jnp.float32) + 1.0)
                        sent = jnp.where(source_ref[t] >= 0, code, sent)
                    msgs[step, f, pl.ds(4 * t + q, 1)] = sent
        strips_x[step][peer] = msgs[step, pl.ds(0, 2)]
        if step == 0:
            pl.semaphore_wait(barrier, total - 1)

        def send(kind, source, target, to_band, to_peer):
            pltpu.make_async_remote_copy(
                src_ref=source,
                dst_ref=target.at[peer],
                send_sem=strip_send.at[step, kind],
                recv_sem=strip_recv.at[step, kind],
                device_id=place(to_band, to_peer),
                device_id_type=MESH,
            ).start()

        @pl.when(has_south)
        def _():
            for offset in range(peers):
                to_peer = lax.rem(peer + offset, peers)
                send(1, msgs.at[step, 3], strips_n[step], band + 1, to_peer)

        @pl.when(has_north)
        def _():
            for offset in range(peers):
                to_peer = lax.rem(peer + offset, peers)
                send(2, msgs.at[step, 2], strips_s[step], band - 1, to_peer)

        for offset in range(1, peers):
            to_peer = lax.rem(peer + offset, peers)
            send(0, msgs.at[step, pl.ds(0, 2)], strips_x[step], band, to_peer)

    def inner(i, carry):
        t = i // chunks
        start = pl.multiple_of((i % chunks) * ROWS, ROWS)
        rows = pl.ds(start, ROWS)
        below = pl.ds(start + 1, ROWS)
        eta, u, v, z = prim[0, t, rows], prim[1, t, rows], prim[2, t, rows], bed[t, rows]
        east = [pltpu.roll(x, size - 1, axis=1) for x in (eta, z, u, v)]
        mass, base, press, tang = face_flux(eta, z, u, v, *east)
        inside = lane_id < size - 1
        mass = jnp.where(inside, mass, 0.0)
        far = jnp.where(inside, base + press, 0.0)
        near = jnp.where(inside, base - press, 0.0)
        tang = jnp.where(inside, tang, 0.0)
        tend[0, t, rows] = mass - pltpu.roll(mass, 1, axis=1)
        tend[1, t, rows] = far - pltpu.roll(near, 1, axis=1)
        tend[2, t, rows] = tang - pltpu.roll(tang, 1, axis=1)
        mass, base, press, tang = face_flux(
            eta, z, v, u, prim[0, t, below], bed[t, below], prim[2, t, below], prim[1, t, below]
        )
        into = pl.ds(pl.multiple_of(start + 8, 8), ROWS)
        faces[0, t, into] = mass
        faces[1, t, into] = base + press
        faces[2, t, into] = base - press
        faces[3, t, into] = tang
        return carry

    def wait_strips(step):
        if peers > 1:
            wait_for(strips_x[step], peers - 1, strip_recv.at[step, 0])

        @pl.when(has_north)
        def _():
            wait_for(strips_n[step], peers, strip_recv.at[step, 1])

        @pl.when(has_south)
        def _():
            wait_for(strips_s[step], peers, strip_recv.at[step, 2])

    def rims(step):
        for t in range(slots):
            for f in range(4):
                device = links_ref[t, 0, f]
                linked = device >= 0
                who = lax.rem(jnp.maximum(device, 0), peers)
                slot = jnp.maximum(links_ref[t, 1, f], 0)
                rows = pl.ds(4 * slot, 4)
                if f < 2:
                    remote = strips_x[step][who, 1 - f, rows]
                else:
                    remote = (strips_n if f == 2 else strips_s)[step][who, rows]
                row = pl.ds(f * slots + t, 1)
                if step == 0:
                    told = remote[3:4]
                    level = told
                    for r in range(bands):
                        edge = edge_in[r * peers + who, pl.ds((1, 0, 3, 2)[f], 1)]
                        level = jnp.where(told == CODE * (r + 1.0), edge, level)
                    ghost[3, row] = jnp.where(linked, level, own[3, row])
                for q in range(3):
                    mine = own[q, row]
                    if q == (1 if f < 2 else 2):
                        mine = -mine
                    ghost[q, row] = jnp.where(linked, remote[q : q + 1], mine)
        row_id = lax.broadcasted_iota(jnp.int32, (4 * slots, size), 0) // slots
        near_side = row_id % 2 == 0
        across = row_id < 2
        g = [ghost[q] for q in range(4)]
        o = [own[q] for q in range(4)]

        def ordered(x):
            h, u, v, z = x
            return h + z, z, jnp.where(across, u, v), jnp.where(across, v, u)

        go, oo = ordered(g), ordered(o)
        left = [jnp.where(near_side, a, b) for a, b in zip(go, oo)]
        right = [jnp.where(near_side, b, a) for a, b in zip(go, oo)]
        mass, base, press, tang = face_flux(*left, *right)
        normal = jnp.where(near_side, base - press, base + press)

        def pick(value, f, t):
            return value[f * slots + t : f * slots + t + 1]

        for t in range(slots):
            for q, value in enumerate((mass, normal, tang)):
                rim[t, pl.ds(2 * q, 1)] = pick(value, 1, t)
                rim[t, pl.ds(2 * q + 1, 1)] = -pick(value, 0, t)
            top, low = pl.ds(7, 1), pl.ds(7 + size, 1)
            faces[0, t, top] = pick(mass, 2, t)
            faces[2, t, top] = pick(normal, 2, t)
            faces[3, t, top] = pick(tang, 2, t)
            faces[0, t, low] = pick(mass, 3, t)
            faces[1, t, low] = pick(normal, 3, t)
            faces[3, t, low] = pick(tang, 3, t)
            rim_t[t] = jnp.transpose(rim[t])

    def update(step, i, carry):
        last = step == STEPS - 1
        current = state_ref if step == 0 else fields
        t = i // chunks
        start = pl.multiple_of((i % chunks) * ROWS, ROWS)
        rows = pl.ds(start, ROWS)
        here = pl.ds(pl.multiple_of(start + 8, 8), ROWS)
        above = pl.ds(start + 7, ROWS)
        turned = rim_t[t, rows]
        border = (lane_id == 0) | (lane_id == size - 1)

        def sides(q):
            return jnp.where(border, pltpu.roll(turned, size - 1 - 2 * q, axis=1), 0.0)

        ratio = 0.5 * DT / CELL
        h = current[0, t, rows] - ratio * (
            tend[0, t, rows] + sides(0) + (faces[0, t, here] - faces[0, t, above])
        )
        qx = current[1, t, rows] - ratio * (
            tend[1, t, rows] + sides(1) + (faces[3, t, here] - faces[3, t, above])
        )
        qy = current[2, t, rows] - ratio * (
            tend[2, t, rows] + sides(2) + (faces[1, t, here] - faces[2, t, above])
        )
        power = jnp.exp((-7.0 / 3.0) * jnp.log(h))
        damp = 1.0 / (1.0 + drag[t, rows] * root(qx * qx + qy * qy) * power)
        qx = qx * damp
        qy = qy * damp
        if last:
            live = t < wet_ref[0]
            out_ref[0, t, rows] = jnp.where(live, h, 0.0)
            out_ref[1, t, rows] = jnp.where(live, qx, 0.0)
            out_ref[2, t, rows] = jnp.where(live, qy, 0.0)
        else:
            fields[0, t, rows] = h
            fields[1, t, rows] = qx
            fields[2, t, rows] = qy
            inv = 1.0 / h
            u = qx * inv
            v = qy * inv
            prim[0, t, rows] = h + bed[t, rows]
            prim[1, t, rows] = u
            prim[2, t, rows] = v
            value = edge_columns(t, rows, 0, h, jnp.zeros_like(h))
            value = edge_columns(t, rows, 1, u, value)
            columns[t, rows] = edge_columns(t, rows, 2, v, value)
        return carry

    def send_terrain():
        def send_edges(to_band, to_peer):
            pltpu.make_async_remote_copy(
                src_ref=edge_msgs.at[to_band],
                dst_ref=edge_in.at[me],
                send_sem=terrain_send.at[2],
                recv_sem=terrain_recv.at[2],
                device_id=place(to_band, to_peer),
                device_id_type=MESH,
            ).start()

        each_other(send_edges)
        for part, (source, target) in enumerate(((out_bed, in_bed), (out_rough, in_rough))):
            for offset in range(1, bands):
                to_band = lax.rem(band + offset, bands)
                pltpu.make_async_remote_copy(
                    src_ref=source.at[to_band],
                    dst_ref=target.at[band],
                    send_sem=terrain_send.at[part],
                    recv_sem=terrain_recv.at[part],
                    device_id=place(to_band, peer),
                    device_id_type=MESH,
                ).start()

    def fill_bed():
        wait_for(in_bed, bands - 1, terrain_recv.at[0])
        for t in range(slots):
            fetched = in_bed[jnp.maximum(source_ref[t], 0)].astype(jnp.float32)
            level = jnp.where(source_ref[t] >= 0, fetched, local_ref[0, t].astype(jnp.float32))
            bed[t, pl.ds(0, size)] = level
            prim[0, t, pl.ds(0, size)] = level + state_ref[0, t]
            own[3, pl.ds(2 * slots + t, 1)] = level[0:1]
            own[3, pl.ds(3 * slots + t, 1)] = level[size - 1 : size]

    def own_edges():
        wait_for(edge_in, total - 1, terrain_recv.at[2])
        for t in range(slots):
            holder = jnp.maximum(source_ref[t], 0) * peers + peer
            for f in range(2):
                row = pl.ds(f * slots + t, 1)
                edge = edge_in[holder, pl.ds(f, 1)]
                own[3, row] = jnp.where(source_ref[t] >= 0, edge, own[3, row])

    def fill_drag():
        wait_for(in_rough, bands - 1, terrain_recv.at[1])
        for t in range(slots):
            fetched = in_rough[jnp.maximum(source_ref[t], 0)].astype(jnp.float32)
            rough = jnp.where(source_ref[t] >= 0, fetched, local_ref[1, t].astype(jnp.float32))
            drag[t] = (DT * GRAVITY) * rough * rough

    for step in range(STEPS):
        send_strips(step)
        if step == 0:
            send_terrain()
            fill_bed()
        lax.fori_loop(0, slots * chunks, inner, 0, unroll=True)
        wait_strips(step)
        if step == 0:
            own_edges()
        rims(step)
        if step == 0:
            fill_drag()
        lax.fori_loop(0, slots * chunks, functools.partial(update, step), 0, unroll=True)

    wait_for(edge_in, total - 1, terrain_send.at[2])
    wait_for(out_rough, bands - 1, terrain_send.at[1])
    wait_for(out_bed, bands - 1, terrain_send.at[0])
    for step in range(STEPS):
        wait_for(strips_x[step], peers - 1, strip_send.at[step, 0])

        @pl.when(has_south)
        def _():
            wait_for(strips_n[step], peers, strip_send.at[step, 1])

        @pl.when(has_north)
        def _():
            wait_for(strips_s[step], peers, strip_send.at[step, 2])


def local(sizes, state, terrain_local, terrain_store, wet_count, face_links, new_source, store_target):
    bands, subs, lanes, slots, size = sizes
    peers = subs * lanes
    f32, bf16 = jnp.float32, jnp.bfloat16
    block = (bands, size, size)
    hbm = pl.BlockSpec(memory_space=pltpu.HBM)
    vmem = pl.BlockSpec(memory_space=pltpu.VMEM)
    msg = (4 * slots, size)
    return pl.pallas_call(
        functools.partial(kernel, sizes),
        out_shape=pltpu.VMEM(state.shape, f32),
        in_specs=[hbm] * 7,
        out_specs=vmem,
        scratch_shapes=[
            pltpu.SMEM(wet_count.shape, jnp.int32),
            pltpu.SMEM(face_links.shape, jnp.int32),
            pltpu.SMEM(new_source.shape, jnp.int32),
            pltpu.SMEM(store_target.shape, jnp.int32),
            pltpu.VMEM(state.shape, f32),
            pltpu.VMEM(terrain_local.shape, bf16),
            pltpu.VMEM(terrain_store.shape, bf16),
            pltpu.VMEM(block, bf16),
            pltpu.VMEM(block, bf16),
            pltpu.VMEM(block, bf16),
            pltpu.VMEM(block, bf16),
            pltpu.VMEM((slots, size + 8, size), f32),
            pltpu.VMEM((slots, size, size), f32),
            pltpu.VMEM((3, slots, size, size), f32),
            pltpu.VMEM((3, slots, size + 8, size), f32),
            pltpu.VMEM((4, slots, size + 16, size), f32),
            pltpu.VMEM((3, slots, size, size), f32),
            pltpu.VMEM((slots, size, size), f32),
            pltpu.VMEM((slots, size, size), f32),
            pltpu.VMEM((slots, size, size), f32),
            pltpu.VMEM((4,) + msg, f32),
            pltpu.VMEM((4,) + msg, f32),
            pltpu.VMEM((STEPS, 4) + msg, f32),
            [pltpu.VMEM((peers, 2) + msg, f32) for _ in range(STEPS)],
            [pltpu.VMEM((peers,) + msg, f32) for _ in range(STEPS)],
            [pltpu.VMEM((peers,) + msg, f32) for _ in range(STEPS)],
            pltpu.VMEM((bands, 4, size), f32),
            pltpu.VMEM((bands * peers, 4, size), f32),
            pltpu.SemaphoreType.DMA((7,)),
            pltpu.SemaphoreType.DMA((3,)),
            pltpu.SemaphoreType.DMA((3,)),
            pltpu.SemaphoreType.DMA((STEPS, 3)),
            pltpu.SemaphoreType.DMA((STEPS, 3)),
        ],
        compiler_params=pltpu.CompilerParams(
            collective_id=0, has_side_effects=True, vmem_limit_bytes=63 * 1024 * 1024
        ),
    )(wet_count, face_links, new_source, store_target, state, terrain_local, terrain_store)


def solution(mesh):
    shape = mesh.shape
    devices = P(None, AXES, None, None)
    flat = P(AXES)

    def whole(state, *rest):
        def part(block, *others):
            sizes = (shape["tile"], shape["sub"], shape["lane"], block.shape[1], block.shape[2])
            return local(sizes, block, *others)

        return jax.shard_map(
            part,
            mesh=mesh,
            in_specs=(devices, devices, devices, flat, P(AXES, None, None), flat, flat),
            out_specs=devices,
            check_vma=False,
        )(state, *rest)

    return whole
```
